32 devices in a mesh: dp: 4 (over z), section: 2 (over core), tensor: 4 (over y, x).
Axes of the slice: x: 2, y: 2, z: 4, core: 2. Of those that a mesh axis runs over, the one named last changes fastest.
Arguments:
- tokens: bfloat16 [1024, 2048], P('dp'), may hold values from -6 to 6
- base_rows: int32 [16], replicated, may hold values from 1 to 48, as said below
- baseline_owner: int32 [16], replicated, may hold values from 0 to 3, as said below
- cotangent: bfloat16 [2, 2048, 2048], P('section', 'dp'), may hold values from -6 to 6
- pre_gain: float32 [2, 2048], P('section'), may hold values from 0.25 to 1.75
- input_proj: bfloat16 [2, 2048, 2048], P('section', None, 'tensor'), may hold values from -0.125 to 0.125
- gate_proj: bfloat16 [2, 2048, 2048], P('section', None, 'tensor'), may hold values from -0.125 to 0.125
- state_proj: bfloat16 [2, 2048, 256], P('section'), may hold values from -0.125 to 0.125
- step_proj: bfloat16 [2, 2048, 32], P('section', None, 'tensor'), may hold values from -0.125 to 0.125
- step_bias: float32 [2, 32], P('section', 'tensor'), may hold values from -6 to -1.5
- decay_log: float32 [2, 32], P('section', 'tensor'), may hold values from 0 to 2.5
- skip_gain: float32 [2, 32], P('section', 'tensor'), may hold values from 0.5 to 1.5
- norm_gain: float32 [2, 2048], P('section', 'tensor'), may hold values from 0.25 to 1.75
- out_proj: bfloat16 [2, 2048, 2048], P('section', 'tensor'), may hold values from -0.125 to 0.125
Outputs:
- activations: bfloat16 [2, 2048, 2048], P('section', 'dp')
- out_grad: bfloat16 [2, 2048, 2048], P('section', 'tensor', 'dp')
The draws below stay inside these ranges and needn't reach their ends.
Inputs may be any that keep to these rules, and one draw needn't show every extreme that they name: `base_rows`: over all baselines they sum to 256; some baseline has exactly 48. `baseline_owner`: every owner holds exactly 4 baselines; the base_rows of one owner's baselines sum to at most 128, and for some owner to exactly 128.
All inputs are finite; a program needn't handle non-finite values.
Results may differ from the reference program's by a relative error of at most 0.025.
Values may be sent and summed in bfloat16 or wider, within the bound.
No kernel may reach another device: no remote copies, remote signals or barrier semaphores. Data moves between devices by JAX's collectives and lax.ppermute only.
A program may use at most 128 MiB of HBM per device.

```python
import jax
import jax.numpy as jnp
from jax import lax

D = 2048
HEADS = 32
HEADDIM = 64
NSTATE = 128
BLOCK = 64
TOK_DEV = 256
TOKENS = 1024
SPAN = 16
PACK = 4
ROWS_OWN = 512
STREAM = 2048
INNER = 2048
OWNERS = 4
N_DP = 4


def pack_layout(key):
    groups = OWNERS // 4
    unit = PACK * SPAN
    half = unit // 2
    longest = 3 * SPAN
    key_load, key_order, key_move, key_perm = jax.random.split(key, 4)
    extra = jax.random.randint(key_load, (groups, 2), 0, unit // 4 + 1, dtype=jnp.int32)
    sorted_loads = jnp.stack([jnp.full((groups,), 2 * unit, jnp.int32), half + extra[:, 0], half + extra[:, 1], unit - extra[:, 0] - extra[:, 1]], axis=1)
    order = jax.vmap(lambda sub: jax.random.permutation(sub, 4))(jax.random.split(key_order, groups))
    loads = jnp.take_along_axis(sorted_loads, order, axis=1).reshape(OWNERS)
    busiest = (order == 0).reshape(OWNERS)
    even_part = loads // PACK
    remainder = loads % PACK
    parts = even_part[:, None] + (jnp.arange(PACK, dtype=jnp.int32)[None, :] < remainder[:, None]).astype(jnp.int32)
    first = parts[:, 0::2]
    second = parts[:, 1::2]
    upper = jnp.minimum(second - 1, longest - first)
    lower = -jnp.minimum(first - 1, longest - second)
    moved_rows = jax.random.randint(key_move, first.shape, lower, upper + 1, dtype=jnp.int32)
    forced = busiest[:, None] & (jnp.arange(PACK // 2, dtype=jnp.int32)[None, :] == 0)
    moved_rows = jnp.where(forced, upper, moved_rows)
    first = first + moved_rows
    second = second - moved_rows
    parts = jnp.stack([first, second], axis=2).reshape(OWNERS * PACK).astype(jnp.int32)
    shuffle = jax.random.permutation(key_perm, OWNERS * PACK)
    rows_each = jnp.zeros((OWNERS * PACK,), jnp.int32).at[shuffle].set(parts)
    owner_each = jnp.zeros((OWNERS * PACK,), jnp.int32).at[shuffle].set((jnp.arange(OWNERS * PACK, dtype=jnp.int32) // PACK).astype(jnp.int32))
    return (rows_each, owner_each)


def draw_base_rows(key, part):
    return pack_layout(jax.random.fold_in(key, 11))[0]


def draw_baseline_owner(key, part):
    return pack_layout(jax.random.fold_in(key, 11))[1]


def strengthened(values, rng, source, target, shards_of, factor):
    owner, partner = [(jnp.arange(values.shape[axis_at]) // (values.shape[axis_at] // shards_of)).reshape([-1 if axis == axis_at else 1 for axis in range(values.ndim)]) for axis_at in (source, target)]
    chosen = jax.random.permutation(rng, shards_of)[partner]
    strong = (owner == chosen) | (owner == (partner + shards_of // 2) % shards_of)
    return jnp.where(strong, factor * values, values)


def shard_levels(key, dims, shards, low, largest):
    def one(axis_at, blocks):
        heights = jax.random.uniform(jax.random.fold_in(jax.random.fold_in(key, 6), axis_at), (blocks,), jnp.float32, low / len(shards), largest / len(shards))
        return jnp.repeat(jnp.exp(heights), dims[axis_at] // blocks).reshape((-1,) + (1,) * (len(dims) - axis_at - 1))

    gain = one(*shards[0])
    for cut in shards[1:]:
        gain = gain * one(*cut)
    return gain


def centred(rng, dims, scale, most, cuts=(), held_as=jnp.bfloat16):
    level = shard_levels(rng, dims, cuts, -0.22, 0.18) if cuts else 1.0
    drawn = jax.random.normal(rng, dims, jnp.float32) * scale * level
    return jnp.minimum(jnp.maximum(drawn, -most), most).astype(held_as)


def heavy_noise(stream_key, dims, deviation, most, cuts, heavy, kind=jnp.bfloat16):
    drawn = deviation * jax.random.normal(stream_key, dims, jnp.float32)
    if cuts:
        drawn = drawn * shard_levels(stream_key, dims, cuts, -0.22, 0.18)
    return jnp.clip(strengthened(drawn, jax.random.fold_in(stream_key, 3), *heavy), -most, most).astype(kind)


def setup_inputs(seed: int = 0) -> dict:
    key_of = jax.random.split(jax.random.key(seed), 15)
    return {
        "tokens": centred(key_of[0], (TOKENS, D), 1.0, 6.0, ((0, 4),)),
        "base_rows": draw_base_rows(jax.random.fold_in(key_of[14], 71), 0),
        "baseline_owner": draw_baseline_owner(jax.random.fold_in(key_of[14], 71), 0),
        "cotangent": heavy_noise(key_of[3], (2, STREAM, D), 1.0, 6.0, ((0, 2), (1, 4)), (1, 2, 4, 2.0)),
        "pre_gain": jnp.clip(1.0 + 0.15 * jax.random.normal(key_of[4], (2, D), jnp.float32), 0.25, 1.75),
        "input_proj": centred(key_of[5], (2, D, INNER), D ** -0.5, 0.125, ((0, 2), (2, 4))),
        "gate_proj": centred(key_of[6], (2, D, INNER), D ** -0.5, 0.125, ((0, 2), (2, 4))),
        "state_proj": centred(key_of[7], (2, D, 2 * NSTATE), D ** -0.5, 0.125, ((0, 2),)),
        "step_proj": centred(key_of[8], (2, D, HEADS), D ** -0.5, 0.125, ((0, 2), (2, 4))),
        "step_bias": jnp.clip(-6.0 + 4.5 * jax.random.uniform(key_of[9], (2, HEADS), jnp.float32) ** shard_levels(key_of[9], (2, HEADS), ((0, 2), (1, 4)), -0.2, 0.2), -6.0, -1.5),
        "decay_log": jnp.clip(2.5 * jax.random.uniform(key_of[10], (2, HEADS), jnp.float32) ** shard_levels(key_of[10], (2, HEADS), ((0, 2), (1, 4)), -0.2, 0.2), 0.0, 2.5),
        "skip_gain": jnp.clip(0.5 + 1.0 * jax.random.uniform(key_of[11], (2, HEADS), jnp.float32) ** shard_levels(key_of[11], (2, HEADS), ((0, 2), (1, 4)), -0.2, 0.2), 0.5, 1.5),
        "norm_gain": jnp.clip(1.0 + 0.15 * jax.random.normal(key_of[12], (2, INNER), jnp.float32), 0.25, 1.75),
        "out_proj": centred(key_of[13], (2, INNER, D), INNER ** -0.5, 0.125, ((0, 2), (1, 4))),
    }


EPS = 1e-05
HIGH = lax.Precision.HIGHEST

def layout_tables(base_rows, baseline_owner):
    count = base_rows.shape[0]
    index = jnp.arange(count, dtype=jnp.int32)
    ends = jnp.cumsum(base_rows).astype(jnp.int32)
    starts = (ends - base_rows).astype(jnp.int32)
    earlier = (baseline_owner[:, None] == baseline_owner[None, :]) & (index[None, :] < index[:, None])
    owner_start = lax.optimization_barrier(jnp.sum(jnp.where(earlier, base_rows[None, :], 0), axis=1)).astype(jnp.int32)
    return (index, starts, ends, owner_start)

def block_scan(heads_in, b_rows, c_rows, step_size, decay_rate, segment, state, prev_segment, block):
    total_rows, head_count, head_dim = heads_in.shape
    blocks = total_rows // block

    def advance(carried_in, item):
        state_now, segment_before = carried_in
        x_blk, b_blk, c_blk, dt_blk, seg_blk = item
        running = jnp.cumsum(dt_blk * decay_rate[None, :], axis=0)
        positions = jnp.arange(block, dtype=jnp.int32)
        together = (seg_blk[:, None] == seg_blk[None, :]) & (positions[:, None] >= positions[None, :])
        spread = jnp.minimum(running[:, None, :] - running[None, :, :], 0.0)
        decay_mask = jnp.where(together[:, :, None], jnp.exp(spread), 0.0)
        scores = jnp.dot(c_blk, b_blk.T, preferred_element_type=jnp.float32)
        weights = (decay_mask * scores[:, :, None] * dt_blk[None, :, :]).astype(jnp.bfloat16)
        within = jnp.einsum('ijh,jhp->ihp', weights.astype(jnp.float32), x_blk.astype(jnp.float32), precision=HIGH)
        keep_in = (seg_blk == segment_before).astype(jnp.float32)
        state_low = lax.optimization_barrier(state_now.astype(jnp.bfloat16)).astype(jnp.float32)
        readout = jnp.einsum('in,hpn->ihp', c_blk.astype(jnp.float32), state_low, precision=HIGH)
        from_state = keep_in[:, None, None] * jnp.exp(running)[:, :, None] * readout
        last_segment = seg_blk[-1]
        tail_weight = jnp.where((seg_blk == last_segment)[:, None], jnp.exp(running[-1][None, :] - running), 0.0) * dt_blk
        scaled = (tail_weight[:, :, None] * x_blk.astype(jnp.float32)).astype(jnp.bfloat16)
        scaled = lax.optimization_barrier(scaled).astype(jnp.float32)
        fresh_term = jnp.einsum('jhp,jn->hpn', scaled, b_blk.astype(jnp.float32), precision=HIGH)
        keep_state = (last_segment == segment_before).astype(jnp.float32)
        state_next = keep_state * jnp.exp(running[-1])[:, None, None] * state_now + fresh_term
        return ((state_next, last_segment), within + from_state)
    scanned = (heads_in.reshape(blocks, block, head_count, head_dim), b_rows.reshape(blocks, block, -1), c_rows.reshape(blocks, block, -1), step_size.reshape(blocks, block, head_count), segment.reshape(blocks, block))
    (state, prev_segment), outputs = lax.scan(advance, (state, prev_segment), scanned)
    return (outputs.reshape(total_rows, head_count, head_dim), state, prev_segment)

def block_layer(rows_in, segment, params):
    pre_gain, input_proj, gate_proj, state_proj, step_proj, step_bias, decay_log, skip_gain, norm_gain, out_proj = params
    row_count = rows_in.shape[0]
    rows_f = rows_in.astype(jnp.float32)
    normed = (rows_f * lax.rsqrt(lax.optimization_barrier(jnp.mean(rows_f * rows_f, axis=-1, keepdims=True)) + EPS) * pre_gain).astype(jnp.bfloat16)
    scan_in = jax.nn.silu(jnp.dot(normed, input_proj, preferred_element_type=jnp.float32)).astype(jnp.bfloat16)
    gate_pre = jnp.dot(normed, gate_proj, preferred_element_type=jnp.float32)
    state_io = jax.nn.silu(jnp.dot(normed, state_proj, preferred_element_type=jnp.float32)).astype(jnp.bfloat16)
    step_size = jax.nn.softplus(jnp.dot(normed, step_proj, preferred_element_type=jnp.float32) + step_bias)
    decay_rate = -jnp.exp(decay_log)
    heads_in = scan_in.reshape(row_count, HEADS, HEADDIM)
    state_start = jnp.zeros((HEADS, HEADDIM, NSTATE), jnp.float32)
    scan_out, state_end, segment_end = block_scan(heads_in, state_io[:, :NSTATE], state_io[:, NSTATE:], step_size, decay_rate, segment, state_start, jnp.array(-1, jnp.int32), BLOCK)
    scan_out = scan_out + skip_gain[None, :, None] * heads_in.astype(jnp.float32)
    gated = scan_out.reshape(row_count, HEADS * HEADDIM) * jax.nn.silu(gate_pre)
    sq_sum = lax.optimization_barrier(jnp.sum(gated * gated, axis=-1, keepdims=True))
    y_norm = (gated * lax.rsqrt(sq_sum / (HEADS * HEADDIM) + EPS) * norm_gain).astype(jnp.bfloat16)
    result = (rows_f + jnp.dot(y_norm, out_proj, preferred_element_type=jnp.float32)).astype(jnp.bfloat16)
    return (result, y_norm)

def reference(tokens, base_rows, baseline_owner, cotangent, pre_gain, input_proj, gate_proj, state_proj, step_proj, step_bias, decay_log, skip_gain, norm_gain, out_proj):
    index, starts, ends, owner_start = layout_tables(base_rows, baseline_owner)
    local = jnp.arange(TOK_DEV, dtype=jnp.int32)
    inside = ((starts[None, :] <= local[:, None]) & (local[:, None] < ends[None, :])).astype(jnp.int32)
    row_id = lax.optimization_barrier(jnp.sum(inside * index[None, :], axis=1)).astype(jnp.int32)
    row_start = lax.optimization_barrier(jnp.sum(inside * starts[None, :], axis=1)).astype(jnp.int32)
    row_len = lax.optimization_barrier(jnp.sum(inside * base_rows[None, :], axis=1)).astype(jnp.int32)
    row_owner = lax.optimization_barrier(jnp.sum(inside * baseline_owner[None, :], axis=1)).astype(jnp.int32)
    row_ostart = lax.optimization_barrier(jnp.sum(inside * owner_start[None, :], axis=1)).astype(jnp.int32)
    reader = jnp.arange(N_DP, dtype=jnp.int32)[:, None]
    target = row_owner[None, :] * ROWS_OWN + OWNERS * row_ostart[None, :] + reader * row_len[None, :] + (local - row_start)[None, :]
    target = target.reshape(TOKENS).astype(jnp.int32)
    stream = jnp.zeros((STREAM, D), jnp.bfloat16).at[target].set(tokens).reshape(N_DP, ROWS_OWN, D)
    ids_all = jnp.tile(row_id, N_DP).astype(jnp.int32)
    slot_ids = jnp.full((STREAM,), -1, jnp.int32).at[target].set(ids_all).reshape(N_DP, ROWS_OWN)
    starts_flag = jnp.concatenate([jnp.ones((N_DP, 1), jnp.int32), (slot_ids[:, 1:] != slot_ids[:, :-1]).astype(jnp.int32)], axis=1)
    segment = jnp.cumsum(starts_flag, axis=1).astype(jnp.int32)
    everything = (pre_gain, input_proj, gate_proj, state_proj, step_proj, step_bias, decay_log, skip_gain, norm_gain, out_proj)
    enc_params = tuple((item[0] for item in everything))
    dec_params = tuple((item[1] for item in everything))
    cot_all = cotangent.reshape(2, N_DP, ROWS_OWN, D)

    def per_owner(totals, item):
        rows_in, seg_own, cot_enc, cot_dec = item
        latent, y_enc = block_layer(rows_in, seg_own, enc_params)
        rebuilt, y_dec = block_layer(latent, seg_own, dec_params)
        grad_enc = jnp.dot(y_enc.T, cot_enc, preferred_element_type=jnp.float32)
        grad_dec = jnp.dot(y_dec.T, cot_dec, preferred_element_type=jnp.float32)
        return ((totals[0] + grad_enc, totals[1] + grad_dec), (latent, rebuilt))
    zero_grad = jnp.zeros((HEADS * HEADDIM, D), jnp.float32)
    (grad_enc, grad_dec), (latents, rebuilts) = lax.scan(per_owner, (zero_grad, zero_grad), (stream, segment, cot_all[0], cot_all[1]))
    activations = jnp.stack([latents.reshape(STREAM, D), rebuilts.reshape(STREAM, D)])
    out_grad = jnp.stack([grad_enc, grad_dec]).astype(jnp.bfloat16)
    return (activations, out_grad)
```

```python
import functools

import jax
import jax.numpy as jnp
from jax import lax
from jax.experimental import pallas as pl
from jax.experimental.pallas import tpu as pltpu
from jax.sharding import PartitionSpec as P

HEADDIM = 64
NSTATE = 128
MICRO = 2
TILE = 128
EXTRA = 16
EPS = 1e-05
LOG2E = 1.4426950408889634
F32 = jnp.float32
BF16 = jnp.bfloat16
VMEM_LIMIT = 48 * 1024 * 1024

NN = (((1,), (0,)), ((), ()))
NT = (((1,), (1,)), ((), ()))
TN = (((0,), (0,)), ((), ()))


def mm(a, b, dims=NN):
    return lax.dot_general(a, b, dims, preferred_element_type=F32)


def split3(value):
    high = value.astype(BF16)
    rest = value - high.astype(F32)
    mid = rest.astype(BF16)
    low = (rest - mid.astype(F32)).astype(BF16)
    return high, mid, low


def silu(x):
    return x * (1.0 / (1.0 + jnp.exp(-x)))


def iota(shape, axis):
    return lax.broadcasted_iota(jnp.int32, shape, axis)


def vmem():
    return pl.BlockSpec(memory_space=pltpu.VMEM)


def smem():
    return pl.BlockSpec(memory_space=pltpu.SMEM)


def params():
    return pltpu.CompilerParams(vmem_limit_bytes=VMEM_LIMIT)


def cost(flops, moved):
    return pl.CostEstimate(flops=int(flops), bytes_accessed=int(moved), transcendentals=0)


def walk_baselines(rows_ref, owner_ref, count_ref, dp_count, visit):
    for owner in range(dp_count):
        count_ref[owner] = 0

    def step(b, start):
        owner = owner_ref[b]
        length = rows_ref[b]
        owner_start = count_ref[owner]
        visit(b, owner, length, start, owner_start)
        count_ref[owner] = owner_start + length
        return start + length

    lax.fori_loop(0, rows_ref.shape[0], step, jnp.int32(0))


def select_kernel(dp_count, cap, pos_ref, rows_ref, owner_ref, tokens_ref, *refs):
    outs, (slot_ref, count_ref) = refs[:dp_count], refs[dp_count:]
    me, part = pos_ref[0], pos_ref[1]
    tok_rows = tokens_ref.shape[0]
    width = outs[0].shape[1]
    local = iota((8, tok_rows), 1)
    slot_ref[...] = jnp.full((8, tok_rows), -1, jnp.int32)

    def visit(b, owner, length, start, owner_start):
        inside = (local >= start) & (local < start + length)
        slot_ref[...] = jnp.where(inside, local + (owner * cap + owner_start - start), slot_ref[...])

    walk_baselines(rows_ref, owner_ref, count_ref, dp_count, visit)
    columns = tokens_ref[:, pl.ds(pl.multiple_of(part * width, width), width)]
    slots = slot_ref[0:1, :]
    for k in range(dp_count):
        owner = lax.rem(me + k, dp_count)
        chosen = (iota((cap, tok_rows), 0) + owner * cap) == slots
        outs[k][...] = mm(chosen.astype(F32).astype(BF16), columns).astype(BF16)


def place_kernel(dp_count, cap, pos_ref, rows_ref, owner_ref, *refs):
    arrived = refs[:dp_count]
    outs = refs[dp_count : dp_count + MICRO]
    seg_ref, slot_ref, count_ref, packed_ref = refs[dp_count + MICRO :]
    me = pos_ref[0]
    own_slots = seg_ref.shape[0]
    arrival = iota((8, own_slots), 1)
    turn = arrival // cap
    place = arrival - turn * cap
    sender = lax.rem(me - turn + dp_count, dp_count)
    slot_ref[...] = jnp.full((8, own_slots), -1, jnp.int32)
    position = iota((own_slots, TILE), 0)
    seg_ref[...] = jnp.zeros((own_slots, TILE), jnp.int32)

    def visit(b, owner, length, start, owner_start):
        @pl.when(owner == me)
        def _():
            inside = (place >= owner_start) & (place < owner_start + length)
            slot = dp_count * owner_start + sender * length + place - owner_start
            slot_ref[...] = jnp.where(inside, slot, slot_ref[...])
            seg_ref[...] = jnp.where(
                position >= dp_count * owner_start, dp_count * owner_start, seg_ref[...]
            )

    walk_baselines(rows_ref, owner_ref, count_ref, dp_count, visit)
    filled = dp_count * count_ref[me]
    seg_ref[...] = jnp.where(position >= filled, filled, seg_ref[...])
    for k in range(dp_count):
        packed_ref[k * cap : (k + 1) * cap, :] = arrived[k][...]
    micro_rows = own_slots // MICRO
    for m in range(MICRO):
        chosen = (iota((micro_rows, own_slots), 0) + m * micro_rows) == slot_ref[0:1, :]
        outs[m][...] = mm(chosen.astype(F32).astype(BF16), packed_ref[...]).astype(BF16)


def layer_kernel(micro, tensor, band, pos_ref, *refs):
    (blocks, refs) = (refs[:tensor], refs[tensor:])
    (seg_ref, gain_ref, win_ref, wgate_ref, wstate_ref, wstep_ref, bias_ref, decay_ref) = refs[:8]
    (skip_ref, ngain_ref, wout_ref) = refs[8:11]
    refs = refs[11:]
    prev = None
    if micro > 0:
        prev, refs = refs[:4], refs[4:]
    outs, refs = refs[:tensor], refs[tensor:]
    gn_ref, xdt_ref, b_ref, cumt_ref, a_ref = refs[:5]
    normed_ref, xs_ref, z_ref, c_ref, y_ref = refs[5:]
    part = pos_ref[1]
    rows, width = blocks[0].shape
    inner = win_ref.shape[1]
    depth = width * tensor
    square = jnp.zeros((rows, 1), F32)
    for block in blocks:
        value = block[...].astype(F32)
        square = square + jnp.sum(value * value, axis=1, keepdims=True)
    scale = lax.rsqrt(square * (1.0 / depth) + EPS)
    for k, block in enumerate(blocks):
        columns = pl.ds(pl.multiple_of((part ^ k) * width, width), width)
        normed_ref[:, columns] = (block[...].astype(F32) * scale * gain_ref[:, columns]).astype(BF16)
    normed = normed_ref[...]
    state_io = silu(mm(normed, wstate_ref[...])).astype(BF16)
    b_ref[...] = state_io[:, :NSTATE]
    c_ref[...] = state_io[:, NSTATE:]
    pre = mm(normed, wstep_ref[...]) + bias_ref[...]
    step = jnp.maximum(pre, 0.0) + jnp.log1p(jnp.exp(-jnp.abs(pre)))
    heads = inner // HEADDIM
    xs = silu(mm(normed, win_ref[...])).astype(BF16)
    xs_ref[...] = xs
    spread = (iota((TILE, inner), 1) // HEADDIM == iota((TILE, inner), 0)).astype(F32).astype(BF16)
    step_wide = sum(mm(piece, spread) for piece in split3(step))
    xdt_ref[...] = (step_wide * xs.astype(F32)).astype(BF16)
    z_ref[...] = mm(normed, wgate_ref[...])
    a_ref[...] = step * (jnp.exp(decay_ref[...]) * (-LOG2E))

    tiles = rows // TILE
    first = micro * tiles

    def key_rows(ref_now, ref_before, tile):
        if tile >= first:
            return ref_now[(tile - first) * TILE : (tile - first + 1) * TILE, :]
        return ref_before[(tile - first + tiles) * TILE : (tile - first + tiles + 1) * TILE, :]

    before = prev if prev is not None else (None,) * 4
    lane = iota((TILE, TILE), 1)
    low_half = lane < HEADDIM
    nothing = jnp.zeros((TILE, TILE), BF16)
    for q in range(first, first + tiles):
        here = (q - first) * TILE
        keys = [k for k in range(max(0, q - band), q + 1)]
        seg = seg_ref[here : here + TILE, :]
        row_at = iota((TILE, TILE), 0) + q * TILE
        c_rows = c_ref[here : here + TILE, :]
        scores = []
        cum = jnp.zeros((TILE, TILE), F32)
        for k in keys:
            at = lane + k * TILE
            valid = at >= seg
            if k == q:
                valid = valid & (at <= row_at)
            scores.append(jnp.where(valid, mm(c_rows, key_rows(b_ref, before[1], k), NT), 0.0))
            ones = jnp.where(valid, 1.0, 0.0).astype(BF16)
            for piece in split3(key_rows(a_ref, before[3], k)):
                cum = cum + mm(ones, piece)
        cumt_ref[here : here + TILE, :] = cum.T
        cum_rows = [key_rows(cumt_ref, before[2], k) for k in keys]
        for pair in range(heads // 2):
            total = jnp.zeros((TILE, TILE), F32)
            for half in range(2):
                h = 2 * pair + half
                own = jnp.broadcast_to(cum[:, h : h + 1], (TILE, TILE))
                for k, score, cum_row in zip(keys, scores, cum_rows):
                    weight = jnp.exp2(jnp.minimum(own - cum_row[h : h + 1, :], 0.0)) * score
                    x_rows = key_rows(xdt_ref, before[0], k)[:, pair * TILE : (pair + 1) * TILE]
                    keep = low_half if half == 0 else ~low_half
                    x_rows = jnp.where(keep, x_rows, nothing)
                    total = total + mm(weight.astype(BF16), x_rows)
            y_ref[here : here + TILE, pair * TILE : (pair + 1) * TILE] = total

    gated = (y_ref[...] + skip_ref[...] * xs_ref[...].astype(F32)) * silu(z_ref[...])
    sq = gated * gated
    sq_high = sq.astype(BF16)
    sq_low = (sq - sq_high.astype(F32)).astype(BF16)
    ones = jnp.ones((EXTRA, inner), BF16)
    sums = mm(ones, sq_high, NT) + mm(ones, sq_low, NT)
    high, mid, low = split3(sums)
    row = iota(sums.shape, 0)
    zero = jnp.zeros(sums.shape, F32)
    message = jnp.where(
        row == 0,
        high.astype(F32),
        jnp.where(row == 1, mid.astype(F32), jnp.where(row == 2, low.astype(F32), zero)),
    ).astype(BF16)
    gn = (gated * ngain_ref[...]).astype(BF16)
    gn_ref[...] = gn
    for k, out in enumerate(outs):
        columns = pl.ds(pl.multiple_of((part ^ k) * width, width), width)
        out[0:rows, :] = mm(gn, wout_ref[:, columns]).astype(BF16)
        out[rows : rows + EXTRA, :] = jnp.zeros((EXTRA, width), BF16)
        out[rows : rows + EXTRA, 0:rows] = message


def sum_kernel(tensor, inner_all, *refs):
    parts, (residual_ref, gn_ref, out_ref, y_ref) = refs[:tensor], refs[tensor:]
    rows, width = residual_ref.shape
    ones = jnp.ones((EXTRA, TILE), BF16)
    square = sum(mm(part[rows : rows + EXTRA, 0:rows], ones, TN) for part in parts)
    scale = lax.rsqrt(square * (1.0 / inner_all) + EPS)
    for c in range(0, width, TILE):
        total = sum(part[0:rows, c : c + TILE].astype(F32) for part in parts)
        out_ref[:, c : c + TILE] = (
            residual_ref[:, c : c + TILE].astype(F32) + total * scale
        ).astype(BF16)
    for c in range(0, gn_ref.shape[1], TILE):
        y_ref[:, c : c + TILE] = (gn_ref[:, c : c + TILE].astype(F32) * scale).astype(BF16)


def grad_kernel(dp_count, pos_ref, *refs):
    ys, (cot_ref,), outs = refs[:MICRO], refs[MICRO : MICRO + 1], refs[MICRO + 1 :]
    me = pos_ref[0]
    rows = ys[0].shape[0]
    width = outs[0].shape[1]
    for k, out in enumerate(outs):
        columns = pl.ds(pl.multiple_of(lax.rem(me + k, dp_count) * width, width), width)
        total = 0.0
        for m in range(MICRO):
            total = total + mm(ys[m][...], cot_ref[m * rows : (m + 1) * rows, columns], TN)
        out[...] = total.astype(BF16)


def whole_grad_kernel(*refs):
    ys, (cot_ref, out_ref) = refs[:MICRO], refs[MICRO:]
    rows = ys[0].shape[0]
    total = 0.0
    for m in range(MICRO):
        total = total + mm(ys[m][...], cot_ref[m * rows : (m + 1) * rows, :], TN)
    out_ref[...] = total.astype(BF16)


def assemble_kernel(tensor, pos_ref, *refs):
    out_ref = refs[-1]
    part = pos_ref[1]
    for m in range(MICRO):
        for k in range(tensor):
            block = refs[m * tensor + k]
            rows, width = block.shape
            columns = pl.ds(pl.multiple_of((part ^ k) * width, width), width)
            out_ref[0, m * rows : (m + 1) * rows, columns] = block[...]


def tensor_exchange(values, sections):
    count = lax.axis_size("tensor")
    return [values[0]] + [
        lax.ppermute(
            values[k],
            ("section", "tensor"),
            [(s * count + t, s * count + (t ^ k)) for s in sections for t in range(count)],
        )
        for k in range(1, count)
    ]


def dp_exchange(values, section):
    count = lax.axis_size("dp")
    return [values[0]] + [
        lax.ppermute(
            values[k],
            ("dp", "section"),
            [(d * 2 + section, (d + k) % count * 2 + section) for d in range(count)],
        )
        for k in range(1, count)
    ]


def hand_over(value):
    count = lax.axis_size("tensor")
    return [
        lax.ppermute(value, ("section", "tensor"), [(t, count + (t ^ k)) for t in range(count)])
        for k in range(count)
    ]


def per_device(
    tokens,
    base_rows,
    baseline_owner,
    cotangent,
    pre_gain,
    input_proj,
    gate_proj,
    state_proj,
    step_proj,
    step_bias,
    decay_log,
    skip_gain,
    norm_gain,
    out_proj,
):
    dp_count = lax.axis_size("dp")
    tensor = lax.axis_size("tensor")
    tok_rows, feat = tokens.shape
    cap = 2 * tok_rows // dp_count
    own_slots = cap * dp_count
    width = feat // tensor
    micro_rows = own_slots // MICRO
    inner = input_proj.shape[2]
    heads = step_proj.shape[2]
    longest = 3 * tok_rows // base_rows.shape[0] * dp_count
    band = (longest - 1 + TILE - 1) // TILE
    dp_at = lax.axis_index("dp")
    section = lax.axis_index("section")
    pos = jnp.stack([dp_at, lax.axis_index("tensor")]).astype(jnp.int32)
    shape = jax.ShapeDtypeStruct
    tables = (pos, base_rows, baseline_owner)

    outgoing = pl.pallas_call(
        functools.partial(select_kernel, dp_count, cap),
        out_shape=[shape((cap, width), BF16)] * dp_count,
        in_specs=[smem()] * 3 + [vmem()],
        out_specs=[vmem()] * dp_count,
        scratch_shapes=[pltpu.VMEM((8, tok_rows), jnp.int32), pltpu.SMEM((dp_count,), jnp.int32)],
        compiler_params=params(),
        name="select_rows",
    )(*tables, tokens)
    arrived = dp_exchange(outgoing, 0)
    *own_blocks, seg = pl.pallas_call(
        functools.partial(place_kernel, dp_count, cap),
        out_shape=[shape((micro_rows, width), BF16)] * MICRO + [shape((own_slots, TILE), jnp.int32)],
        in_specs=[smem()] * 3 + [vmem()] * dp_count,
        out_specs=[vmem()] * (MICRO + 1),
        scratch_shapes=[
            pltpu.VMEM((8, own_slots), jnp.int32),
            pltpu.SMEM((dp_count,), jnp.int32),
            pltpu.VMEM((own_slots, width), BF16),
        ],
        compiler_params=params(),
        name="place_rows",
    )(*tables, *arrived)

    def lanes(value):
        return jnp.pad(value, ((0, 0), (0, TILE - heads)))

    weights = (
        pre_gain,
        input_proj[0],
        gate_proj[0],
        state_proj[0],
        lanes(step_proj[0]),
        lanes(step_bias),
        lanes(decay_log),
        jnp.repeat(skip_gain, HEADDIM, axis=1),
        norm_gain,
        out_proj[0],
    )

    def layer(micro, blocks, carried):
        seg_part = seg[micro * micro_rows : (micro + 1) * micro_rows]
        prev = () if micro == 0 else carried
        got = pl.pallas_call(
            functools.partial(layer_kernel, micro, tensor, band),
            out_shape=[shape((micro_rows + EXTRA, width), BF16)] * tensor
            + [
                shape((micro_rows, inner), BF16),
                shape((micro_rows, inner), BF16),
                shape((micro_rows, NSTATE), BF16),
                shape((micro_rows, TILE), F32),
                shape((micro_rows, TILE), F32),
            ],
            in_specs=[smem()] + [vmem()] * (tensor + 1 + len(weights) + len(prev)),
            out_specs=[vmem()] * (tensor + 5),
            scratch_shapes=[
                pltpu.VMEM((micro_rows, feat), BF16),
                pltpu.VMEM((micro_rows, inner), BF16),
                pltpu.VMEM((micro_rows, inner), F32),
                pltpu.VMEM((micro_rows, NSTATE), BF16),
                pltpu.VMEM((micro_rows, inner), F32),
            ],
            compiler_params=params(),
            cost_estimate=cost(2 * micro_rows * feat * (3 * inner + 512), 12e6),
            name="layer_part",
        )(pos, *blocks, seg_part, *weights, *prev)
        parts, gn, carry = got[:tensor], got[tensor], got[tensor + 1 :]
        return parts, gn, carry

    def finish(parts, residual, gn):
        return pl.pallas_call(
            functools.partial(sum_kernel, tensor, inner * tensor),
            out_shape=[shape((micro_rows, width), BF16), shape((micro_rows, inner), BF16)],
            in_specs=[vmem()] * (tensor + 2),
            out_specs=[vmem()] * 2,
            compiler_params=params(),
            cost_estimate=cost(1e6, 3e6),
            name="sum_parts",
        )(*parts, residual, gn)

    def block(sources, active):
        results, ys, carried = [], [], None
        for micro in range(MICRO):
            parts, gn, carried = layer(micro, sources[micro], carried)
            parts = tensor_exchange(parts, (active,))
            result, y = finish(parts, sources[micro][0], gn)
            results.append(result)
            ys.append(y)
        return results, ys

    def gradient(ys, active):
        grad_width = feat // dp_count
        direct = grad_width % TILE == 0
        out_shape = [shape((inner, grad_width), BF16)] * dp_count if direct else [shape((inner, feat), BF16)]
        kernel = functools.partial(grad_kernel, dp_count) if direct else whole_grad_kernel
        head = (pos,) if direct else ()
        got = pl.pallas_call(
            kernel,
            out_shape=out_shape,
            in_specs=[smem()] * len(head) + [vmem()] * (MICRO + 1),
            out_specs=[vmem()] * len(out_shape),
            compiler_params=params(),
            cost_estimate=cost(2 * own_slots * inner * feat, 5e6),
            name="gradient_terms",
        )(*head, *ys, cotangent[0])
        if not direct:
            return lax.psum_scatter(got[0], "dp", scatter_dimension=1, tiled=True)
        terms = dp_exchange(got, active)
        return sum(term.astype(F32) for term in terms).astype(BF16)

    sources = [tensor_exchange([own] * tensor, (0,)) for own in own_blocks]
    latent, enc_ys = block(sources, 0)
    enc_grad = gradient(enc_ys, 0)
    rebuilt, dec_ys = block([hand_over(value) for value in latent], 1)
    dec_grad = gradient(dec_ys, 1)
    first = section == 0
    finals = []
    for micro in range(MICRO):
        own = jnp.where(first, latent[micro], rebuilt[micro])
        finals.extend(tensor_exchange([own] * tensor, (0, 1)))
    activations = pl.pallas_call(
        functools.partial(assemble_kernel, tensor),
        out_shape=shape((1, own_slots, feat), BF16),
        in_specs=[smem()] + [vmem()] * len(finals),
        out_specs=vmem(),
        compiler_params=params(),
        cost_estimate=cost(1e6, 4e6),
        name="assemble_rows",
    )(pos, *finals)
    return activations, jnp.where(first, enc_grad, dec_grad)[None]


def solution(mesh):
    return jax.shard_map(
        per_device,
        mesh=mesh,
        in_specs=(
            P("dp", None),
            P(),
            P(),
            P("section", "dp", None),
            P("section", None),
            P("section", None, "tensor"),
            P("section", None, "tensor"),
            P("section", None, None),
            P("section", None, "tensor"),
            P("section", "tensor"),
            P("section", "tensor"),
            P("section", "tensor"),
            P("section", "tensor"),
            P("section", "tensor", None),
        ),
        out_specs=(P("section", "dp", None), P("section", "tensor", "dp")),
        check_vma=False,
    )
```

```python
import functools

import jax
import jax.numpy as jnp
from jax import lax
from jax.experimental import pallas as pl
from jax.experimental.pallas import tpu as pltpu
from jax.sharding import PartitionSpec as P

HEADDIM = 64
NSTATE = 128
TILE = 128
EXTRA = 16
EPS = 1e-05
LOG2E = 1.4426950408889634
F32 = jnp.float32
BF16 = jnp.bfloat16
VMEM_LIMIT = 48 * 1024 * 1024

NN = (((1,), (0,)), ((), ()))
NT = (((1,), (1,)), ((), ()))
TN = (((0,), (0,)), ((), ()))


def mm(a, b, dims=NN):
    return lax.dot_general(a, b, dims, preferred_element_type=F32)


def split3(value):
    high = value.astype(BF16)
    rest = value - high.astype(F32)
    mid = rest.astype(BF16)
    low = (rest - mid.astype(F32)).astype(BF16)
    return high, mid, low


def silu(x):
    return x * (1.0 / (1.0 + jnp.exp(-x)))


def iota(shape, axis):
    return lax.broadcasted_iota(jnp.int32, shape, axis)


def vmem():
    return pl.BlockSpec(memory_space=pltpu.VMEM)


def smem():
    return pl.BlockSpec(memory_space=pltpu.SMEM)


def params():
    return pltpu.CompilerParams(vmem_limit_bytes=VMEM_LIMIT)


def cost(flops, moved):
    return pl.CostEstimate(flops=int(flops), bytes_accessed=int(moved), transcendentals=0)


def walk_baselines(rows_ref, owner_ref, count_ref, dp_count, visit):
    for owner in range(dp_count):
        count_ref[owner] = 0

    def step(b, start):
        owner = owner_ref[b]
        length = rows_ref[b]
        owner_start = count_ref[owner]
        visit(b, owner, length, start, owner_start)
        count_ref[owner] = owner_start + length
        return start + length

    lax.fori_loop(0, rows_ref.shape[0], step, jnp.int32(0))


def select_kernel(dp_count, cap, pos_ref, rows_ref, owner_ref, tokens_ref, *refs):
    outs, (slot_ref, count_ref) = refs[:dp_count], refs[dp_count:]
    me, part = pos_ref[0], pos_ref[1]
    tok_rows = tokens_ref.shape[0]
    width = outs[0].shape[1]
    local = iota((8, tok_rows), 1)
    slot_ref[...] = jnp.full((8, tok_rows), -1, jnp.int32)

    def visit(b, owner, length, start, owner_start):
        inside = (local >= start) & (local < start + length)
        slot_ref[...] = jnp.where(inside, local + (owner * cap + owner_start - start), slot_ref[...])

    walk_baselines(rows_ref, owner_ref, count_ref, dp_count, visit)
    columns = tokens_ref[:, pl.ds(pl.multiple_of(part * width, width), width)]
    slots = slot_ref[0:1, :]
    for k in range(dp_count):
        owner = me ^ k
        chosen = (iota((cap, tok_rows), 0) + owner * cap) == slots
        outs[k][...] = mm(chosen.astype(F32).astype(BF16), columns).astype(BF16)


def place_kernel(dp_count, cap, pos_ref, rows_ref, owner_ref, *refs):
    arrived = refs[:dp_count]
    out_ref, seg_ref, slot_ref, count_ref, packed_ref = refs[dp_count:]
    me = pos_ref[0]
    own_slots = seg_ref.shape[0]
    arrival = iota((8, own_slots), 1)
    turn = arrival // cap
    place = arrival - turn * cap
    sender = me ^ turn
    slot_ref[...] = jnp.full((8, own_slots), -1, jnp.int32)
    position = iota((own_slots, TILE), 0)
    seg_ref[...] = jnp.zeros((own_slots, TILE), jnp.int32)

    def visit(b, owner, length, start, owner_start):
        @pl.when(owner == me)
        def _():
            inside = (place >= owner_start) & (place < owner_start + length)
            slot = dp_count * owner_start + sender * length + place - owner_start
            slot_ref[...] = jnp.where(inside, slot, slot_ref[...])
            seg_ref[...] = jnp.where(
                position >= dp_count * owner_start, dp_count * owner_start, seg_ref[...]
            )

    walk_baselines(rows_ref, owner_ref, count_ref, dp_count, visit)
    filled = dp_count * count_ref[me]
    seg_ref[...] = jnp.where(position >= filled, filled, seg_ref[...])
    for k in range(dp_count):
        packed_ref[k * cap : (k + 1) * cap, :] = arrived[k][...]
    chosen = iota((own_slots, own_slots), 0) == slot_ref[0:1, :]
    out_ref[...] = mm(chosen.astype(F32).astype(BF16), packed_ref[...]).astype(BF16)


def layer_kernel(active, counts, band, pos_ref, *refs):
    @pl.when(pos_ref[2] == active)
    def _():
        layer_body(counts, band, pos_ref, *refs)


def layer_body(counts, band, pos_ref, *refs):
    blocks = []
    for count in counts:
        blocks.append(refs[:count])
        refs = refs[count:]
    tensor = len(counts)
    (seg_ref, gain_ref, win_ref, wgate_ref, wstate_ref, wstep_ref, bias_ref, decay_ref) = refs[:8]
    (skip_ref, ngain_ref, wout_ref) = refs[8:11]
    outs, refs = refs[11 : 11 + tensor], refs[11 + tensor :]
    normed_ref, xs_ref, z_ref, b_ref, c_ref, a_ref, cumt_ref, xlow_ref, xhigh_ref, y_ref = refs[:10]
    held, sem = refs[10:15], refs[15]
    loads = [
        pltpu.make_async_copy(source, target, sem.at[index])
        for index, (source, target) in enumerate(
            zip((wstate_ref, wstep_ref, win_ref, wgate_ref, wout_ref), held)
        )
    ]
    for load in loads:
        load.start()
    wstate_ref, wstep_ref, win_ref, wgate_ref, wout_ref = held
    part = pos_ref[1]
    rows, width = seg_ref.shape[0], blocks[0][0].shape[1]
    inner = win_ref.shape[1]
    depth = width * tensor
    piece_rows = min(block.shape[0] for pieces in blocks for block in pieces)
    for at in range(0, rows, piece_rows):
        chunks = []
        for pieces in blocks:
            height = pieces[0].shape[0]
            start = at % height
            chunks.append(pieces[at // height][start : start + piece_rows, :].astype(F32))
        square = sum(jnp.sum(chunk * chunk, axis=1, keepdims=True) for chunk in chunks)
        scale = lax.rsqrt(square * (1.0 / depth) + EPS)
        for k, chunk in enumerate(chunks):
            columns = pl.ds(pl.multiple_of((part ^ k) * width, width), width)
            normed_ref[at : at + piece_rows, columns] = (
                chunk * scale * gain_ref[:, columns]
            ).astype(BF16)
    normed = normed_ref[...]
    loads[0].wait()
    state_io = silu(mm(normed, wstate_ref[...])).astype(BF16)
    b_ref[...] = state_io[:, :NSTATE]
    c_ref[...] = state_io[:, NSTATE:]
    loads[1].wait()
    pre = mm(normed, wstep_ref[...]) + bias_ref[...]
    step = jnp.maximum(pre, 0.0) + jnp.log1p(jnp.exp(-jnp.abs(pre)))
    heads = inner // HEADDIM
    loads[2].wait()
    xs = silu(mm(normed, win_ref[...])).astype(BF16)
    xs_ref[...] = xs
    spread = (iota((TILE, inner), 1) // HEADDIM == iota((TILE, inner), 0)).astype(F32).astype(BF16)
    step_wide = sum(mm(piece, spread) for piece in split3(step))
    scaled = step_wide * xs.astype(F32)
    low_half = iota(scaled.shape, 1) % TILE < HEADDIM
    xlow_ref[...] = jnp.where(low_half, scaled, 0.0).astype(BF16)
    xhigh_ref[...] = jnp.where(low_half, 0.0, scaled).astype(BF16)
    loads[3].wait()
    z_ref[...] = mm(normed, wgate_ref[...])
    a_ref[...] = step * (jnp.exp(decay_ref[...]) * (-LOG2E))

    lane = iota((TILE, TILE), 1)
    for q in range(rows // TILE):
        here = slice(q * TILE, (q + 1) * TILE)
        keys = [slice(k * TILE, (k + 1) * TILE) for k in range(max(0, q - band), q + 1)]
        seg = seg_ref[here, :]
        row_at = iota((TILE, TILE), 0) + q * TILE
        c_rows = c_ref[here, :]
        scores = []
        cum = jnp.zeros((TILE, TILE), F32)
        for key in keys:
            at = lane + key.start
            valid = (at >= seg) & (at <= row_at)
            scores.append(jnp.where(valid, mm(c_rows, b_ref[key, :], NT), 0.0))
            ones = jnp.where(valid, 1.0, 0.0).astype(BF16)
            for piece in split3(a_ref[key, :]):
                cum = cum + mm(ones, piece)
        cumt_ref[here, :] = cum.T
        for pair in range(heads // 2):
            total = jnp.zeros((TILE, TILE), F32)
            columns = slice(pair * TILE, (pair + 1) * TILE)
            own = [
                jnp.broadcast_to(cum[:, h : h + 1], (TILE, TILE)) for h in (2 * pair, 2 * pair + 1)
            ]
            for key, score in zip(keys, scores):
                weights = [
                    (
                        jnp.exp2(jnp.minimum(own[half] - cumt_ref[key, :][h : h + 1, :], 0.0)) * score
                    ).astype(BF16)
                    for half, h in enumerate((2 * pair, 2 * pair + 1))
                ]
                values = jnp.concatenate([xlow_ref[key, columns], xhigh_ref[key, columns]], axis=0)
                total = total + mm(jnp.concatenate(weights, axis=1), values)
            y_ref[here, columns] = total

    gated = (y_ref[...] + skip_ref[...] * xs_ref[...].astype(F32)) * silu(z_ref[...])
    sq = gated * gated
    sq_high = sq.astype(BF16)
    sq_low = (sq - sq_high.astype(F32)).astype(BF16)
    ones = jnp.ones((EXTRA, inner), BF16)
    sums = mm(ones, sq_high, NT) + mm(ones, sq_low, NT)
    high, mid, low = split3(sums)
    row = iota(sums.shape, 0)
    zero = jnp.zeros(sums.shape, F32)
    message = jnp.where(
        row == 0,
        high.astype(F32),
        jnp.where(row == 1, mid.astype(F32), jnp.where(row == 2, low.astype(F32), zero)),
    ).astype(BF16)
    gn = (gated * ngain_ref[...]).astype(BF16)
    loads[4].wait()
    for k, out in enumerate(outs):
        columns = pl.ds(pl.multiple_of((part ^ k) * width, width), width)
        out[0:rows, :] = mm(gn, wout_ref[:, columns]).astype(BF16)
        out[rows : rows + EXTRA, :] = jnp.zeros((EXTRA, width), BF16)
        out[rows : rows + EXTRA, 0:rows] = message
    tail = rows + EXTRA
    outs[0][tail : tail + rows, :] = gn
    at = tail + rows
    for piece in blocks[0]:
        outs[0][at : at + piece.shape[0], :] = piece[...]
        at += piece.shape[0]


def sum_kernel(tensor, inner_all, rows, *refs):
    parts, (out_ref, y_ref) = refs[:tensor], refs[tensor:]
    width = parts[0].shape[1]
    tail = rows + EXTRA
    ones = jnp.ones((EXTRA, TILE), BF16)
    square = sum(mm(part[rows:tail, 0:rows], ones, TN) for part in parts)
    scale = lax.rsqrt(square * (1.0 / inner_all) + EPS)
    for c in range(0, width, TILE):
        columns = slice(c, c + TILE)
        total = sum(part[0:rows, columns].astype(F32) for part in parts)
        residual = parts[0][tail + rows : tail + 2 * rows, columns].astype(F32)
        out_ref[:, columns] = (residual + total * scale).astype(BF16)
        y_ref[:, columns] = (parts[0][tail : tail + rows, columns].astype(F32) * scale).astype(BF16)


def half_kernel(pos_ref, own_ref, other_ref, out_ref):
    rows = out_ref.shape[0]

    @pl.when(pos_ref[2] == 0)
    def _():
        out_ref[...] = other_ref[rows : 2 * rows, :]

    @pl.when(pos_ref[2] != 0)
    def _():
        out_ref[...] = own_ref[0:rows, :]


def grad_kernel(active, pieces, pos_ref, *refs):
    ys, cot_ref, outs = refs[: -1 - pieces], refs[-1 - pieces], refs[-pieces:]
    width = outs[0].shape[1]

    @pl.when(pos_ref[2] == active)
    def _():
        for k, out in enumerate(outs):
            if pieces == 1:
                columns = slice(0, width)
            else:
                columns = pl.ds(pl.multiple_of((pos_ref[0] ^ k) * width, width), width)
            total, at = 0.0, 0
            for y in ys:
                rows = y.shape[0]
                total = total + mm(y[...], cot_ref[at : at + rows, columns], TN)
                at += rows
            out[...] = total.astype(BF16)


def total_kernel(encoder_count, pos_ref, *refs):
    encoder, decoder, out_ref = refs[:encoder_count], refs[encoder_count:-1], refs[-1]

    def add(terms):
        rows = terms[0].shape[0]
        for at in range(0, rows, TILE):
            total = sum(term[at : at + TILE, :].astype(F32) for term in terms)
            out_ref[0, at : at + TILE, :] = total.astype(BF16)

    @pl.when(pos_ref[2] == 0)
    def _():
        add(encoder)

    @pl.when(pos_ref[2] != 0)
    def _():
        add(decoder)


def assemble_kernel(counts, pos_ref, *refs):
    groups = []
    for count in counts:
        groups.append(refs[:count])
        refs = refs[count:]
    out_ref, sem = refs
    part = pos_ref[1]
    tensor = len(counts) // 2

    def move(blocks):
        copies = []
        for k, pieces in enumerate(blocks):
            at = 0
            for piece in pieces:
                rows, width = piece.shape
                columns = pl.ds(pl.multiple_of((part ^ k) * width, width), width)
                copies.append(
                    pltpu.make_async_copy(
                        piece, out_ref.at[0, at : at + rows, columns], sem.at[len(copies)]
                    )
                )
                at += rows
        for copy in copies:
            copy.start()
        for copy in copies:
            copy.wait()

    @pl.when(pos_ref[2] == 0)
    def _():
        move(groups[:tensor])

    @pl.when(pos_ref[2] != 0)
    def _():
        move(groups[tensor:])


def tensor_gather(value):
    count = lax.axis_size("tensor")
    return [
        lax.ppermute(value, "tensor", [(t, t ^ k) for t in range(count)]) for k in range(1, count)
    ]


def tensor_cross(values, active):
    count = lax.axis_size("tensor")
    other = 1 - active
    return [
        lax.ppermute(
            value,
            ("section", "tensor"),
            [(active * count + t, other * count + (t ^ k)) for t in range(count)]
            + [(other * count + t, active * count + t) for t in range(count)],
        )
        for k, value in enumerate(values)
    ]


def dp_cross(values, active, first):
    count = lax.axis_size("dp")
    other = 1 - active
    return [
        lax.ppermute(
            value,
            ("dp", "section"),
            [(d * 2 + active, (d ^ k) * 2 + other) for d in range(count)]
            + [(d * 2 + other, d * 2 + active) for d in range(count)],
        )
        for k, value in enumerate(values, first)
    ]


def per_device(
    tokens,
    base_rows,
    baseline_owner,
    cotangent,
    pre_gain,
    input_proj,
    gate_proj,
    state_proj,
    step_proj,
    step_bias,
    decay_log,
    skip_gain,
    norm_gain,
    out_proj,
):
    dp_count = lax.axis_size("dp")
    tensor = lax.axis_size("tensor")
    tok_rows, feat = tokens.shape
    cap = 2 * tok_rows // dp_count
    own_slots = cap * dp_count
    width = feat // tensor
    inner = input_proj.shape[2]
    heads = step_proj.shape[2]
    longest = 3 * tok_rows // base_rows.shape[0] * dp_count
    band = (longest - 1 + TILE - 1) // TILE
    dp_at = lax.axis_index("dp")
    section = lax.axis_index("section")
    pos = jnp.stack([dp_at, lax.axis_index("tensor"), section]).astype(jnp.int32)
    shape = jax.ShapeDtypeStruct
    tables = (pos, base_rows, baseline_owner)

    outgoing = pl.pallas_call(
        functools.partial(select_kernel, dp_count, cap),
        out_shape=[shape((cap, width), BF16)] * dp_count,
        in_specs=[smem()] * 3 + [vmem()],
        out_specs=[vmem()] * dp_count,
        scratch_shapes=[pltpu.VMEM((8, tok_rows), jnp.int32), pltpu.SMEM((dp_count,), jnp.int32)],
        compiler_params=params(),
        name="select_rows",
    )(*tables, tokens)
    swap = [(0, 1), (1, 0)]
    barrier = lax.optimization_barrier
    cot_own = cotangent[0]
    cot_other = lax.ppermute(cot_own, "section", swap)
    arrived = [outgoing[0]] + dp_cross(outgoing[1:], 0, 1)
    arrived, cot_other = barrier((arrived, cot_other))
    own_block, seg = pl.pallas_call(
        functools.partial(place_kernel, dp_count, cap),
        out_shape=[shape((own_slots, width), BF16), shape((own_slots, TILE), jnp.int32)],
        in_specs=[smem()] * 3 + [vmem()] * dp_count,
        out_specs=[vmem()] * 2,
        scratch_shapes=[
            pltpu.VMEM((8, own_slots), jnp.int32),
            pltpu.SMEM((dp_count,), jnp.int32),
            pltpu.VMEM((own_slots, width), BF16),
        ],
        compiler_params=params(),
        name="place_rows",
    )(*tables, *arrived)

    def lanes(value):
        return jnp.pad(value, ((0, 0), (0, TILE - heads)))

    weights = (
        pre_gain,
        input_proj[0],
        gate_proj[0],
        state_proj[0],
        lanes(step_proj[0]),
        lanes(step_bias),
        lanes(decay_log),
        jnp.repeat(skip_gain, HEADDIM, axis=1),
        norm_gain,
        out_proj[0],
    )

    is_large = [index in (1, 2, 3, 4, 9) for index in range(len(weights))]
    part_rows = [3 * own_slots + EXTRA] + [own_slots + EXTRA] * (tensor - 1)

    def layer(active, blocks):
        counts = tuple(len(pieces) for pieces in blocks)
        return pl.pallas_call(
            functools.partial(layer_kernel, active, counts, band),
            out_shape=[shape((count, width), BF16) for count in part_rows],
            in_specs=[smem()]
            + [vmem()] * (sum(counts) + 1)
            + [pl.BlockSpec(memory_space=pl.ANY) if large else vmem() for large in is_large],
            out_specs=[vmem()] * tensor,
            scratch_shapes=[
                pltpu.VMEM((own_slots, feat), BF16),
                pltpu.VMEM((own_slots, inner), BF16),
                pltpu.VMEM((own_slots, inner), F32),
                pltpu.VMEM((own_slots, NSTATE), BF16),
                pltpu.VMEM((own_slots, NSTATE), BF16),
                pltpu.VMEM((own_slots, TILE), F32),
                pltpu.VMEM((own_slots, TILE), F32),
                pltpu.VMEM((own_slots, inner), BF16),
                pltpu.VMEM((own_slots, inner), BF16),
                pltpu.VMEM((own_slots, inner), F32),
            ]
            + [pltpu.VMEM(weights[index].shape, BF16) for index in (3, 4, 1, 2, 9)]
            + [pltpu.SemaphoreType.DMA((5,))],
            compiler_params=params(),
            cost_estimate=cost(2 * own_slots * feat * (3 * inner + 512), 12e6),
            name="layer_part",
        )(pos, *[piece for pieces in blocks for piece in pieces], seg, *weights)

    def finish(parts):
        return pl.pallas_call(
            functools.partial(sum_kernel, tensor, inner * tensor, own_slots),
            out_shape=[shape((own_slots, width), BF16), shape((own_slots, inner), BF16)],
            in_specs=[vmem()] * tensor,
            out_specs=[vmem()] * 2,
            compiler_params=params(),
            cost_estimate=cost(1e6, 3e6),
            name="sum_parts",
        )(*parts)

    def gradient_terms(active, ys, cot, pieces):
        return pl.pallas_call(
            functools.partial(grad_kernel, active, pieces),
            out_shape=[shape((inner, feat // pieces), BF16)] * pieces,
            in_specs=[smem()] + [vmem()] * (len(ys) + 1),
            out_specs=[vmem()] * pieces,
            compiler_params=params(),
            cost_estimate=cost(2 * own_slots * inner * feat, 5e6),
            name="gradient_terms",
        )(pos, *ys, cot)

    direct = feat // dp_count % TILE == 0
    pieces = dp_count if direct else 1
    half = own_slots // 2

    blocks = [[value] for value in tensor_cross([own_block] * tensor, 1)]
    latent, enc_y = finish(tensor_cross(layer(0, blocks), 0))

    passed = lax.ppermute(latent, "section", swap)
    mine = pl.pallas_call(
        half_kernel,
        out_shape=shape((half, width), BF16),
        in_specs=[smem()] + [vmem()] * 2,
        out_specs=vmem(),
        compiler_params=params(),
        cost_estimate=cost(1e5, 5e5),
        name="own_half",
    )(pos, latent, passed)
    gathered = tensor_gather(mine)
    enc_y, gathered[0] = barrier((enc_y, gathered[0]))
    enc_terms = gradient_terms(1, [enc_y], cot_other, pieces)
    enc_terms, gathered = barrier((enc_terms, gathered))
    swapped = [lax.ppermute(value, "section", swap) for value in gathered]
    sources = [[latent]] + [[top, bottom] for top, bottom in zip(gathered, swapped)]
    kept = [[passed]] + [[top, bottom] for top, bottom in zip(swapped, gathered)]

    enc_grad, order = [], list(range(dp_count))[::-1] if direct else []

    def send_gradient(count):
        for k in order[:count]:
            enc_grad.extend(dp_cross([enc_terms[k]], 1, k))
        del order[:count]

    sources, enc_terms = barrier((sources, enc_terms))
    send_gradient(1)
    parts = layer(1, sources)
    parts, enc_grad, enc_terms = barrier((parts, enc_grad, enc_terms))
    arrived = tensor_cross(parts, 1)
    send_gradient(1)
    arrived, enc_grad, enc_terms = barrier((arrived, enc_grad, enc_terms))
    send_gradient(dp_count)
    rebuilt, dec_y = finish(arrived)
    dec_terms = gradient_terms(0, [dec_y], cot_other, pieces)
    if direct:
        dec_grad = dp_cross(dec_terms, 0, 0)
    else:
        enc_grad, dec_grad = [
            [
                lax.ppermute(
                    lax.psum_scatter(terms[0], "dp", scatter_dimension=1, tiled=True), "section", swap
                )
            ]
            for terms in (enc_terms, dec_terms)
        ]
    rebuilt, dec_terms = barrier((rebuilt, dec_terms))
    finals = [[value] for value in tensor_cross([rebuilt] * tensor, 0)]

    groups = kept + finals
    counts = tuple(len(group) for group in groups)
    activations = pl.pallas_call(
        functools.partial(assemble_kernel, counts),
        out_shape=shape((1, own_slots, feat), BF16),
        in_specs=[smem()] + [pl.BlockSpec(memory_space=pl.ANY)] * sum(counts),
        out_specs=pl.BlockSpec(memory_space=pl.ANY),
        scratch_shapes=[pltpu.SemaphoreType.DMA((2 * tensor,))],
        compiler_params=params(),
        cost_estimate=cost(1e6, 4e6),
        name="assemble_rows",
    )(pos, *[piece for group in groups for piece in group])
    out_grad = pl.pallas_call(
        functools.partial(total_kernel, len(enc_grad)),
        out_shape=shape((1, inner, feat // dp_count), BF16),
        in_specs=[smem()] + [vmem()] * (len(enc_grad) + len(dec_grad)),
        out_specs=vmem(),
        compiler_params=params(),
        cost_estimate=cost(1e6, 4e6),
        name="gradient_total",
    )(pos, *enc_grad, *dec_grad)
    return activations, out_grad


def solution(mesh):
    return jax.shard_map(
        per_device,
        mesh=mesh,
        in_specs=(
            P("dp", None),
            P(),
            P(),
            P("section", "dp", None),
            P("section", None),
            P("section", None, "tensor"),
            P("section", None, "tensor"),
            P("section", None, None),
            P("section", None, "tensor"),
            P("section", "tensor"),
            P("section", "tensor"),
            P("section", "tensor"),
            P("section", "tensor"),
            P("section", "tensor", None),
        ),
        out_specs=(P("section", "dp", None), P("section", "tensor", "dp")),
        check_vma=False,
    )
```

```python
import functools

import jax
import jax.numpy as jnp
from jax import lax
from jax.experimental import pallas as pl
from jax.experimental.pallas import tpu as pltpu
from jax.sharding import PartitionSpec as P

HEADDIM = 64
NSTATE = 128
TILE = 128
EXTRA = 16
EPS = 1e-05
LOG2E = 1.4426950408889634
F32 = jnp.float32
BF16 = jnp.bfloat16
VMEM_LIMIT = 48 * 1024 * 1024

NN = (((1,), (0,)), ((), ()))
NT = (((1,), (1,)), ((), ()))
TN = (((0,), (0,)), ((), ()))


def mm(a, b, dims=NN):
    return lax.dot_general(a, b, dims, preferred_element_type=F32)


def split3(value):
    high = value.astype(BF16)
    rest = value - high.astype(F32)
    mid = rest.astype(BF16)
    low = (rest - mid.astype(F32)).astype(BF16)
    return high, mid, low


def silu(x):
    return x * (1.0 / (1.0 + jnp.exp(-x)))


def iota(shape, axis):
    return lax.broadcasted_iota(jnp.int32, shape, axis)


def vmem():
    return pl.BlockSpec(memory_space=pltpu.VMEM)


def smem():
    return pl.BlockSpec(memory_space=pltpu.SMEM)


def params():
    return pltpu.CompilerParams(vmem_limit_bytes=VMEM_LIMIT)


def cost(flops, moved):
    return pl.CostEstimate(flops=int(flops), bytes_accessed=int(moved), transcendentals=0)


def walk_baselines(rows_ref, owner_ref, count_ref, dp_count, visit):
    for owner in range(dp_count):
        count_ref[owner] = 0

    def step(b, start):
        owner = owner_ref[b]
        length = rows_ref[b]
        owner_start = count_ref[owner]
        visit(b, owner, length, start, owner_start)
        count_ref[owner] = owner_start + length
        return start + length

    lax.fori_loop(0, rows_ref.shape[0], step, jnp.int32(0))


def select_kernel(dp_count, cap, pos_ref, rows_ref, owner_ref, tokens_ref, *refs):
    outs, (slot_ref, count_ref, held_ref, sem) = refs[:dp_count], refs[dp_count:]
    me, part = pos_ref[0], pos_ref[1]
    tok_rows = tokens_ref.shape[0]
    width = outs[0].shape[1]
    load = pltpu.make_async_copy(
        tokens_ref.at[:, pl.ds(pl.multiple_of(part * width, width), width)], held_ref, sem
    )
    load.start()
    local = iota((8, tok_rows), 1)
    slot_ref[...] = jnp.full((8, tok_rows), -1, jnp.int32)

    def visit(b, owner, length, start, owner_start):
        inside = (local >= start) & (local < start + length)
        slot_ref[...] = jnp.where(inside, local + (owner * cap + owner_start - start), slot_ref[...])

    walk_baselines(rows_ref, owner_ref, count_ref, dp_count, visit)
    load.wait()
    columns = held_ref[...]
    slots = slot_ref[0:1, :]
    for k in range(dp_count):
        owner = me ^ k
        chosen = (iota((cap, tok_rows), 0) + owner * cap) == slots
        outs[k][...] = mm(chosen.astype(F32).astype(BF16), columns).astype(BF16)


def place_kernel(dp_count, cap, pos_ref, rows_ref, owner_ref, *refs):
    arrived = refs[:dp_count]
    out_ref, seg_ref, slot_ref, count_ref, packed_ref = refs[dp_count:]
    me = pos_ref[0]
    own_slots = seg_ref.shape[0]
    arrival = iota((8, own_slots), 1)
    turn = arrival // cap
    place = arrival - turn * cap
    sender = me ^ turn
    slot_ref[...] = jnp.full((8, own_slots), -1, jnp.int32)
    position = iota((own_slots, TILE), 0)
    seg_ref[...] = jnp.zeros((own_slots, TILE), jnp.int32)

    def visit(b, owner, length, start, owner_start):
        @pl.when(owner == me)
        def _():
            inside = (place >= owner_start) & (place < owner_start + length)
            slot = dp_count * owner_start + sender * length + place - owner_start
            slot_ref[...] = jnp.where(inside, slot, slot_ref[...])
            seg_ref[...] = jnp.where(
                position >= dp_count * owner_start, dp_count * owner_start, seg_ref[...]
            )

    walk_baselines(rows_ref, owner_ref, count_ref, dp_count, visit)
    filled = dp_count * count_ref[me]
    seg_ref[...] = jnp.where(position >= filled, filled, seg_ref[...])
    for k in range(dp_count):
        packed_ref[k * cap : (k + 1) * cap, :] = arrived[k][...]
    chosen = iota((own_slots, own_slots), 0) == slot_ref[0:1, :]
    out_ref[...] = mm(chosen.astype(F32).astype(BF16), packed_ref[...]).astype(BF16)


def layer_kernel(active, counts, band, pos_ref, *refs):
    @pl.when(pos_ref[2] == active)
    def _():
        layer_body(counts, band, pos_ref, *refs)


def layer_body(counts, band, pos_ref, *refs):
    blocks = []
    for count in counts:
        blocks.append(refs[:count])
        refs = refs[count:]
    tensor = len(counts)
    (seg_ref, gain_ref, win_ref, wgate_ref, wstate_ref, wstep_ref, bias_ref, decay_ref) = refs[:8]
    (skip_ref, ngain_ref, wout_ref) = refs[8:11]
    outs, refs = refs[11 : 11 + tensor], refs[11 + tensor :]
    normed_ref, xs_ref, z_ref, b_ref, c_ref, a_ref, cumt_ref, xlow_ref, xhigh_ref, y_ref = refs[:10]
    held, sem = refs[10:15], refs[15]
    loads = [
        pltpu.make_async_copy(source, target, sem.at[index])
        for index, (source, target) in enumerate(
            zip((wstate_ref, wstep_ref, win_ref, wgate_ref, wout_ref), held)
        )
    ]
    for load in loads:
        load.start()
    wstate_ref, wstep_ref, win_ref, wgate_ref, wout_ref = held
    part = pos_ref[1]
    rows, width = seg_ref.shape[0], blocks[0][0].shape[1]
    inner = win_ref.shape[1]
    depth = width * tensor
    piece_rows = min(block.shape[0] for pieces in blocks for block in pieces)
    for at in range(0, rows, piece_rows):
        chunks = []
        for pieces in blocks:
            height = pieces[0].shape[0]
            start = at % height
            chunks.append(pieces[at // height][start : start + piece_rows, :].astype(F32))
        square = sum(jnp.sum(chunk * chunk, axis=1, keepdims=True) for chunk in chunks)
        scale = lax.rsqrt(square * (1.0 / depth) + EPS)
        for k, chunk in enumerate(chunks):
            columns = pl.ds(pl.multiple_of((part ^ k) * width, width), width)
            normed_ref[at : at + piece_rows, columns] = (
                chunk * scale * gain_ref[:, columns]
            ).astype(BF16)
    normed = normed_ref[...]
    loads[0].wait()
    state_io = silu(mm(normed, wstate_ref[...])).astype(BF16)
    b_ref[...] = state_io[:, :NSTATE]
    c_ref[...] = state_io[:, NSTATE:]
    loads[1].wait()
    pre = mm(normed, wstep_ref[...]) + bias_ref[...]
    step = jnp.maximum(pre, 0.0) + jnp.log1p(jnp.exp(-jnp.abs(pre)))
    heads = inner // HEADDIM
    loads[2].wait()
    xs = silu(mm(normed, win_ref[...])).astype(BF16)
    xs_ref[...] = xs
    spread = (iota((TILE, inner), 1) // HEADDIM == iota((TILE, inner), 0)).astype(F32).astype(BF16)
    step_wide = sum(mm(piece, spread) for piece in split3(step))
    scaled = step_wide * xs.astype(F32)
    low_half = iota(scaled.shape, 1) % TILE < HEADDIM
    xlow_ref[...] = jnp.where(low_half, scaled, 0.0).astype(BF16)
    xhigh_ref[...] = jnp.where(low_half, 0.0, scaled).astype(BF16)
    loads[3].wait()
    z_ref[...] = mm(normed, wgate_ref[...])
    a_ref[...] = step * (jnp.exp(decay_ref[...]) * (-LOG2E))

    lane = iota((TILE, TILE), 1)
    for q in range(rows // TILE):
        here = slice(q * TILE, (q + 1) * TILE)
        keys = [slice(k * TILE, (k + 1) * TILE) for k in range(max(0, q - band), q + 1)]
        seg = seg_ref[here, :]
        row_at = iota((TILE, TILE), 0) + q * TILE
        c_rows = c_ref[here, :]
        scores = []
        cum = jnp.zeros((TILE, TILE), F32)
        for key in keys:
            at = lane + key.start
            valid = (at >= seg) & (at <= row_at)
            scores.append(jnp.where(valid, mm(c_rows, b_ref[key, :], NT), 0.0))
            ones = jnp.where(valid, 1.0, 0.0).astype(BF16)
            for piece in split3(a_ref[key, :]):
                cum = cum + mm(ones, piece)
        cumt_ref[here, :] = cum.T
        for pair in range(heads // 2):
            total = jnp.zeros((TILE, TILE), F32)
            columns = slice(pair * TILE, (pair + 1) * TILE)
            own = [
                jnp.broadcast_to(cum[:, h : h + 1], (TILE, TILE)) for h in (2 * pair, 2 * pair + 1)
            ]
            for key, score in zip(keys, scores):
                weights = [
                    (
                        jnp.exp2(jnp.minimum(own[half] - cumt_ref[key, :][h : h + 1, :], 0.0)) * score
                    ).astype(BF16)
                    for half, h in enumerate((2 * pair, 2 * pair + 1))
                ]
                values = jnp.concatenate([xlow_ref[key, columns], xhigh_ref[key, columns]], axis=0)
                total = total + mm(jnp.concatenate(weights, axis=1), values)
            y_ref[here, columns] = total

    gated = (y_ref[...] + skip_ref[...] * xs_ref[...].astype(F32)) * silu(z_ref[...])
    sq = gated * gated
    sq_high = sq.astype(BF16)
    sq_low = (sq - sq_high.astype(F32)).astype(BF16)
    ones = jnp.ones((EXTRA, inner), BF16)
    sums = mm(ones, sq_high, NT) + mm(ones, sq_low, NT)
    high, mid, low = split3(sums)
    row = iota(sums.shape, 0)
    zero = jnp.zeros(sums.shape, F32)
    message = jnp.where(
        row == 0,
        high.astype(F32),
        jnp.where(row == 1, mid.astype(F32), jnp.where(row == 2, low.astype(F32), zero)),
    ).astype(BF16)
    gn = (gated * ngain_ref[...]).astype(BF16)
    loads[4].wait()
    for k, out in enumerate(outs):
        columns = pl.ds(pl.multiple_of((part ^ k) * width, width), width)
        out[0:rows, :] = mm(gn, wout_ref[:, columns]).astype(BF16)
        out[rows : rows + EXTRA, :] = jnp.zeros((EXTRA, width), BF16)
        out[rows : rows + EXTRA, 0:rows] = message
    tail = rows + EXTRA
    outs[0][tail : tail + rows, :] = gn
    at = tail + rows
    for piece in blocks[0]:
        outs[0][at : at + piece.shape[0], :] = piece[...]
        at += piece.shape[0]


def sum_kernel(tensor, inner_all, rows, *refs):
    parts, outs, y_ref = refs[:tensor], refs[tensor:-1], refs[-1]
    width = parts[0].shape[1]
    tail = rows + EXTRA
    ones = jnp.ones((EXTRA, TILE), BF16)
    square = sum(mm(part[rows:tail, 0:rows], ones, TN) for part in parts)
    scale = lax.rsqrt(square * (1.0 / inner_all) + EPS)
    for c in range(0, width, TILE):
        columns = slice(c, c + TILE)
        total = sum(part[0:rows, columns].astype(F32) for part in parts)
        residual = parts[0][tail + rows : tail + 2 * rows, columns].astype(F32)
        result = (residual + total * scale).astype(BF16)
        size = rows // len(outs)
        for index, out_ref in enumerate(outs):
            out_ref[:, columns] = result[index * size : (index + 1) * size, :]
        y_ref[:, columns] = (parts[0][tail : tail + rows, columns].astype(F32) * scale).astype(BF16)


def half_kernel(pos_ref, own_ref, other_ref, out_ref):
    @pl.when(pos_ref[2] == 0)
    def _():
        out_ref[...] = other_ref[...]

    @pl.when(pos_ref[2] != 0)
    def _():
        out_ref[...] = own_ref[...]


def grad_kernel(active, pieces, pos_ref, *refs):
    ys, cot_ref, outs = refs[: -1 - pieces], refs[-1 - pieces], refs[-pieces:]
    width = outs[0].shape[1]

    @pl.when(pos_ref[2] == active)
    def _():
        for k, out in enumerate(outs):
            if pieces == 1:
                columns = slice(0, width)
            else:
                columns = pl.ds(pl.multiple_of((pos_ref[0] ^ k) * width, width), width)
            total, at = 0.0, 0
            for y in ys:
                rows = y.shape[0]
                total = total + mm(y[...], cot_ref[at : at + rows, columns], TN)
                at += rows
            out[...] = total.astype(BF16)


def total_kernel(encoder_count, pos_ref, *refs):
    encoder, decoder, out_ref = refs[:encoder_count], refs[encoder_count:-1], refs[-1]

    def add(terms):
        rows = terms[0].shape[0]
        for at in range(0, rows, TILE):
            total = sum(term[at : at + TILE, :].astype(F32) for term in terms)
            out_ref[0, at : at + TILE, :] = total.astype(BF16)

    @pl.when(pos_ref[2] == 0)
    def _():
        add(encoder)

    @pl.when(pos_ref[2] != 0)
    def _():
        add(decoder)


def assemble_kernel(counts, pos_ref, *refs):
    groups = []
    for count in counts:
        groups.append(refs[:count])
        refs = refs[count:]
    out_ref, sem = refs
    part = pos_ref[1]
    tensor = len(counts) // 2

    def move(blocks):
        copies = []
        for k, pieces in enumerate(blocks):
            at = 0
            for piece in pieces:
                rows, width = piece.shape
                columns = pl.ds(pl.multiple_of((part ^ k) * width, width), width)
                copies.append(
                    pltpu.make_async_copy(
                        piece, out_ref.at[0, at : at + rows, columns], sem.at[len(copies)]
                    )
                )
                at += rows
        for copy in copies:
            copy.start()
        for copy in copies:
            copy.wait()

    @pl.when(pos_ref[2] == 0)
    def _():
        move(groups[:tensor])

    @pl.when(pos_ref[2] != 0)
    def _():
        move(groups[tensor:])


def tensor_gather(value):
    count = lax.axis_size("tensor")
    return [
        lax.ppermute(value, "tensor", [(t, t ^ k) for t in range(count)]) for k in range(1, count)
    ]


def tensor_cross(values, active, first=0):
    count = lax.axis_size("tensor")
    other = 1 - active
    return [
        lax.ppermute(
            value,
            ("section", "tensor"),
            [(active * count + t, other * count + (t ^ k)) for t in range(count)]
            + [(other * count + t, active * count + t) for t in range(count)],
        )
        for k, value in enumerate(values, first)
    ]


def dp_cross(values, active, first):
    count = lax.axis_size("dp")
    other = 1 - active
    return [
        lax.ppermute(
            value,
            ("dp", "section"),
            [(d * 2 + active, (d ^ k) * 2 + other) for d in range(count)]
            + [(d * 2 + other, d * 2 + active) for d in range(count)],
        )
        for k, value in enumerate(values, first)
    ]


def per_device(
    tokens,
    base_rows,
    baseline_owner,
    cotangent,
    pre_gain,
    input_proj,
    gate_proj,
    state_proj,
    step_proj,
    step_bias,
    decay_log,
    skip_gain,
    norm_gain,
    out_proj,
):
    dp_count = lax.axis_size("dp")
    tensor = lax.axis_size("tensor")
    tok_rows, feat = tokens.shape
    cap = 2 * tok_rows // dp_count
    own_slots = cap * dp_count
    width = feat // tensor
    inner = input_proj.shape[2]
    heads = step_proj.shape[2]
    longest = 3 * tok_rows // base_rows.shape[0] * dp_count
    band = (longest - 1 + TILE - 1) // TILE
    dp_at = lax.axis_index("dp")
    section = lax.axis_index("section")
    pos = jnp.stack([dp_at, lax.axis_index("tensor"), section]).astype(jnp.int32)
    shape = jax.ShapeDtypeStruct
    tables = (pos, base_rows, baseline_owner)

    outgoing = pl.pallas_call(
        functools.partial(select_kernel, dp_count, cap),
        out_shape=[shape((cap, width), BF16)] * dp_count,
        in_specs=[smem()] * 3 + [pl.BlockSpec(memory_space=pl.ANY)],
        out_specs=[vmem()] * dp_count,
        scratch_shapes=[
            pltpu.VMEM((8, tok_rows), jnp.int32),
            pltpu.SMEM((dp_count,), jnp.int32),
            pltpu.VMEM((tok_rows, width), BF16),
            pltpu.SemaphoreType.DMA,
        ],
        compiler_params=params(),
        name="select_rows",
    )(*tables, tokens)
    swap = [(0, 1), (1, 0)]
    barrier = lax.optimization_barrier
    cot_own = cotangent[0]
    cot_other = lax.ppermute(cot_own, "section", swap)
    arrived = [outgoing[0]] + dp_cross(outgoing[1:], 0, 1)
    arrived, cot_other = barrier((arrived, cot_other))
    own_block, seg = pl.pallas_call(
        functools.partial(place_kernel, dp_count, cap),
        out_shape=[shape((own_slots, width), BF16), shape((own_slots, TILE), jnp.int32)],
        in_specs=[smem()] * 3 + [vmem()] * dp_count,
        out_specs=[vmem()] * 2,
        scratch_shapes=[
            pltpu.VMEM((8, own_slots), jnp.int32),
            pltpu.SMEM((dp_count,), jnp.int32),
            pltpu.VMEM((own_slots, width), BF16),
        ],
        compiler_params=params(),
        name="place_rows",
    )(*tables, *arrived)

    def lanes(value):
        return jnp.pad(value, ((0, 0), (0, TILE - heads)))

    weights = (
        pre_gain,
        input_proj[0],
        gate_proj[0],
        state_proj[0],
        lanes(step_proj[0]),
        lanes(step_bias),
        lanes(decay_log),
        jnp.repeat(skip_gain, HEADDIM, axis=1),
        norm_gain,
        out_proj[0],
    )

    is_large = [index in (1, 2, 3, 4, 9) for index in range(len(weights))]
    part_rows = [3 * own_slots + EXTRA] + [own_slots + EXTRA] * (tensor - 1)

    def layer(active, blocks):
        counts = tuple(len(pieces) for pieces in blocks)
        return pl.pallas_call(
            functools.partial(layer_kernel, active, counts, band),
            out_shape=[shape((count, width), BF16) for count in part_rows],
            in_specs=[smem()]
            + [vmem()] * (sum(counts) + 1)
            + [pl.BlockSpec(memory_space=pl.ANY) if large else vmem() for large in is_large],
            out_specs=[vmem()] * tensor,
            scratch_shapes=[
                pltpu.VMEM((own_slots, feat), BF16),
                pltpu.VMEM((own_slots, inner), BF16),
                pltpu.VMEM((own_slots, inner), F32),
                pltpu.VMEM((own_slots, NSTATE), BF16),
                pltpu.VMEM((own_slots, NSTATE), BF16),
                pltpu.VMEM((own_slots, TILE), F32),
                pltpu.VMEM((own_slots, TILE), F32),
                pltpu.VMEM((own_slots, inner), BF16),
                pltpu.VMEM((own_slots, inner), BF16),
                pltpu.VMEM((own_slots, inner), F32),
            ]
            + [pltpu.VMEM(weights[index].shape, BF16) for index in (3, 4, 1, 2, 9)]
            + [pltpu.SemaphoreType.DMA((5,))],
            compiler_params=params(),
            cost_estimate=cost(2 * own_slots * feat * (3 * inner + 512), 12e6),
            name="layer_part",
        )(pos, *[piece for pieces in blocks for piece in pieces], seg, *weights)

    def finish(parts, count):
        return pl.pallas_call(
            functools.partial(sum_kernel, tensor, inner * tensor, own_slots),
            out_shape=[shape((own_slots // count, width), BF16)] * count
            + [shape((own_slots, inner), BF16)],
            in_specs=[vmem()] * tensor,
            out_specs=[vmem()] * (count + 1),
            compiler_params=params(),
            cost_estimate=cost(1e6, 3e6),
            name="sum_parts",
        )(*parts)

    def gradient_terms(active, ys, cot, pieces):
        return pl.pallas_call(
            functools.partial(grad_kernel, active, pieces),
            out_shape=[shape((inner, feat // pieces), BF16)] * pieces,
            in_specs=[smem()] + [vmem()] * (len(ys) + 1),
            out_specs=[vmem()] * pieces,
            compiler_params=params(),
            cost_estimate=cost(2 * own_slots * inner * feat, 5e6),
            name="gradient_terms",
        )(pos, *ys, cot)

    direct = feat // dp_count % TILE == 0
    pieces = dp_count if direct else 1
    half = own_slots // 2

    blocks = [[value] for value in tensor_cross([own_block] * tensor, 1)]
    top, bottom, enc_y = finish(tensor_cross(layer(0, blocks), 0), 2)

    passed = lax.ppermute(bottom, "section", swap)
    mine = pl.pallas_call(
        half_kernel,
        out_shape=shape((half, width), BF16),
        in_specs=[smem()] + [vmem()] * 2,
        out_specs=vmem(),
        compiler_params=params(),
        cost_estimate=cost(1e5, 5e5),
        name="own_half",
    )(pos, top, passed)
    gathered = tensor_gather(mine)
    enc_y, gathered[0] = barrier((enc_y, gathered[0]))
    enc_terms = gradient_terms(1, [enc_y], cot_other, pieces)
    enc_terms, gathered = barrier((enc_terms, gathered))
    swapped = [lax.ppermute(value, "section", swap) for value in gathered]
    sources = [[top, bottom]] + [list(pair) for pair in zip(gathered, swapped)]
    kept = [list(pair) for pair in zip(swapped, gathered)]

    sources, enc_terms = barrier((sources, enc_terms))
    first = [k for k in range(dp_count) if k != dp_count // 2] if direct else []
    enc_grad = [dp_cross([enc_terms[k]], 1, k)[0] for k in first]
    parts, enc_grad, enc_terms = barrier((layer(1, sources), enc_grad, enc_terms))
    if direct:
        enc_grad = enc_grad + dp_cross([enc_terms[dp_count // 2]], 1, dp_count // 2)
    arrived = tensor_cross(parts, 1)
    top, arrived = barrier((top, arrived))
    kept = [[lax.ppermute(top, "section", swap), passed]] + kept
    rebuilt, dec_y = finish(arrived, 1)
    dec_terms = gradient_terms(0, [dec_y], cot_other, pieces)
    dec_terms, enc_grad = barrier((dec_terms, enc_grad))
    if direct:
        dec_grad = dp_cross(dec_terms, 0, 0)
    else:
        enc_grad, dec_grad = [
            [
                lax.ppermute(
                    lax.psum_scatter(terms[0], "dp", scatter_dimension=1, tiled=True), "section", swap
                )
            ]
            for terms in (enc_terms, dec_terms)
        ]
    rebuilt, dec_terms = barrier((rebuilt, dec_terms))
    finals = tensor_cross([rebuilt] * 2, 0)
    rebuilt, finals[0] = barrier((rebuilt, finals[0]))
    finals = [[value] for value in finals + tensor_cross([rebuilt] * (tensor - 2), 0, 2)]

    groups = kept + finals
    counts = tuple(len(group) for group in groups)
    activations = pl.pallas_call(
        functools.partial(assemble_kernel, counts),
        out_shape=shape((1, own_slots, feat), BF16),
        in_specs=[smem()] + [pl.BlockSpec(memory_space=pl.ANY)] * sum(counts),
        out_specs=pl.BlockSpec(memory_space=pl.ANY),
        scratch_shapes=[pltpu.SemaphoreType.DMA((2 * tensor,))],
        compiler_params=params(),
        cost_estimate=cost(1e6, 4e6),
        name="assemble_rows",
    )(pos, *[piece for group in groups for piece in group])
    out_grad = pl.pallas_call(
        functools.partial(total_kernel, len(enc_grad)),
        out_shape=shape((1, inner, feat // dp_count), BF16),
        in_specs=[smem()] + [vmem()] * (len(enc_grad) + len(dec_grad)),
        out_specs=vmem(),
        compiler_params=params(),
        cost_estimate=cost(1e6, 4e6),
        name="gradient_total",
    )(pos, *enc_grad, *dec_grad)
    return activations, out_grad


def solution(mesh):
    return jax.shard_map(
        per_device,
        mesh=mesh,
        in_specs=(
            P("dp", None),
            P(),
            P(),
            P("section", "dp", None),
            P("section", None),
            P("section", None, "tensor"),
            P("section", None, "tensor"),
            P("section", None, None),
            P("section", None, "tensor"),
            P("section", "tensor"),
            P("section", "tensor"),
            P("section", "tensor"),
            P("section", "tensor"),
            P("section", "tensor", None),
        ),
        out_specs=(P("section", "dp", None), P("section", "tensor", "dp")),
        check_vma=False,
    )
```

```python
import functools

import jax
import jax.numpy as jnp
from jax import lax
from jax.experimental import pallas as pl
from jax.experimental.pallas import tpu as pltpu
from jax.sharding import PartitionSpec as P

HEADDIM = 64
NSTATE = 128
TILE = 128
EXTRA = 16
EPS = 1e-05
LOG2E = 1.4426950408889634
F32 = jnp.float32
BF16 = jnp.bfloat16
VMEM_LIMIT = 45 * 1024 * 1024

NN = (((1,), (0,)), ((), ()))
NT = (((1,), (1,)), ((), ()))
TN = (((0,), (0,)), ((), ()))


def mm(a, b, dims=NN):
    return lax.dot_general(a, b, dims, preferred_element_type=F32)


def split3(value):
    high = value.astype(BF16)
    rest = value - high.astype(F32)
    mid = rest.astype(BF16)
    low = (rest - mid.astype(F32)).astype(BF16)
    return high, mid, low


def silu(x):
    return x * (1.0 / (1.0 + jnp.exp(-x)))


def iota(shape, axis):
    return lax.broadcasted_iota(jnp.int32, shape, axis)


def vmem():
    return pl.BlockSpec(memory_space=pltpu.VMEM)


def smem():
    return pl.BlockSpec(memory_space=pltpu.SMEM)


def params():
    return pltpu.CompilerParams(vmem_limit_bytes=VMEM_LIMIT)


def cost(flops, moved):
    return pl.CostEstimate(flops=int(flops), bytes_accessed=int(moved), transcendentals=0)


def walk_baselines(rows_ref, owner_ref, count_ref, dp_count, visit):
    for owner in range(dp_count):
        count_ref[owner] = 0

    def step(b, start):
        owner = owner_ref[b]
        length = rows_ref[b]
        owner_start = count_ref[owner]
        visit(b, owner, length, start, owner_start)
        count_ref[owner] = owner_start + length
        return start + length

    lax.fori_loop(0, rows_ref.shape[0], step, jnp.int32(0))


def select_kernel(dp_count, cap, pos_ref, rows_ref, owner_ref, tokens_ref, *refs):
    outs, (slot_ref, count_ref, held_ref, sem) = refs[:dp_count], refs[dp_count:]
    me, part = pos_ref[0], pos_ref[1]
    tok_rows = tokens_ref.shape[0]
    width = outs[0].shape[1]
    load = pltpu.make_async_copy(
        tokens_ref.at[:, pl.ds(pl.multiple_of(part * width, width), width)], held_ref, sem
    )
    load.start()
    local = iota((8, tok_rows), 1)
    slot_ref[...] = jnp.full((8, tok_rows), -1, jnp.int32)

    def visit(b, owner, length, start, owner_start):
        inside = (local >= start) & (local < start + length)
        slot_ref[...] = jnp.where(inside, local + (owner * cap + owner_start - start), slot_ref[...])

    walk_baselines(rows_ref, owner_ref, count_ref, dp_count, visit)
    load.wait()
    columns = held_ref[...]
    slots = slot_ref[0:1, :]
    for k in range(dp_count):
        owner = me ^ k
        chosen = (iota((cap, tok_rows), 0) + owner * cap) == slots
        outs[k][...] = mm(chosen.astype(F32).astype(BF16), columns).astype(BF16)


def place_kernel(dp_count, cap, pos_ref, rows_ref, owner_ref, *refs):
    arrived = refs[:dp_count]
    out_ref, seg_ref, slot_ref, count_ref, packed_ref = refs[dp_count:]
    me = pos_ref[0]
    own_slots = seg_ref.shape[0]
    arrival = iota((8, own_slots), 1)
    turn = arrival // cap
    place = arrival - turn * cap
    sender = me ^ turn
    slot_ref[...] = jnp.full((8, own_slots), -1, jnp.int32)
    position = iota((own_slots, TILE), 0)
    seg_ref[...] = jnp.zeros((own_slots, TILE), jnp.int32)

    def visit(b, owner, length, start, owner_start):
        @pl.when(owner == me)
        def _():
            inside = (place >= owner_start) & (place < owner_start + length)
            slot = dp_count * owner_start + sender * length + place - owner_start
            slot_ref[...] = jnp.where(inside, slot, slot_ref[...])
            seg_ref[...] = jnp.where(
                position >= dp_count * owner_start, dp_count * owner_start, seg_ref[...]
            )

    walk_baselines(rows_ref, owner_ref, count_ref, dp_count, visit)
    filled = dp_count * count_ref[me]
    seg_ref[...] = jnp.where(position >= filled, filled, seg_ref[...])
    for k in range(dp_count):
        packed_ref[k * cap : (k + 1) * cap, :] = arrived[k][...]
    chosen = iota((own_slots, own_slots), 0) == slot_ref[0:1, :]
    out_ref[...] = mm(chosen.astype(F32).astype(BF16), packed_ref[...]).astype(BF16)


def layer_kernel(active, counts, band, pos_ref, *refs):
    @pl.when(pos_ref[2] == active)
    def _():
        layer_body(counts, band, pos_ref, *refs)


def layer_body(counts, band, pos_ref, *refs):
    blocks = []
    for count in counts:
        blocks.append(refs[:count])
        refs = refs[count:]
    tensor = len(counts)
    (seg_ref, gain_ref, win_ref, wgate_ref, wstate_ref, wstep_ref, bias_ref, decay_ref) = refs[:8]
    (skip_ref, ngain_ref, wout_ref) = refs[8:11]
    outs, refs = refs[11 : 11 + tensor], refs[11 + tensor :]
    normed_ref, xs_ref, z_ref, b_ref, c_ref, a_ref, cumt_ref, xlow_ref, xhigh_ref, y_ref = refs[:10]
    held, sem = refs[10:15], refs[15]
    loads = [
        pltpu.make_async_copy(source, target, sem.at[index])
        for index, (source, target) in enumerate(
            zip((wstate_ref, wstep_ref, win_ref, wgate_ref, wout_ref), held)
        )
    ]
    for load in loads:
        load.start()
    wstate_ref, wstep_ref, win_ref, wgate_ref, wout_ref = held
    part = pos_ref[1]
    rows, width = seg_ref.shape[0], blocks[0][0].shape[1]
    inner = win_ref.shape[1]
    depth = width * tensor
    piece_rows = min(block.shape[0] for pieces in blocks for block in pieces)
    for at in range(0, rows, piece_rows):
        chunks = []
        for pieces in blocks:
            height = pieces[0].shape[0]
            start = at % height
            chunks.append(pieces[at // height][start : start + piece_rows, :].astype(F32))
        square = sum(jnp.sum(chunk * chunk, axis=1, keepdims=True) for chunk in chunks)
        scale = lax.rsqrt(square * (1.0 / depth) + EPS)
        for k, chunk in enumerate(chunks):
            columns = pl.ds(pl.multiple_of((part ^ k) * width, width), width)
            normed_ref[at : at + piece_rows, columns] = (
                chunk * scale * gain_ref[:, columns]
            ).astype(BF16)
    loads[0].wait()
    state_io = silu(mm(normed_ref[...], wstate_ref[...])).astype(BF16)
    b_ref[...] = state_io[:, :NSTATE]
    c_ref[...] = state_io[:, NSTATE:]
    loads[1].wait()
    pre = mm(normed_ref[...], wstep_ref[...]) + bias_ref[...]
    step = jnp.maximum(pre, 0.0) + jnp.log1p(jnp.exp(-jnp.abs(pre)))
    heads = inner // HEADDIM
    loads[2].wait()
    xs = silu(mm(normed_ref[...], win_ref[...])).astype(BF16)
    xs_ref[...] = xs
    spread = (iota((TILE, inner), 1) // HEADDIM == iota((TILE, inner), 0)).astype(F32).astype(BF16)
    step_wide = sum(mm(piece, spread) for piece in split3(step))
    scaled = step_wide * xs.astype(F32)
    low_half = iota(scaled.shape, 1) % TILE < HEADDIM
    xlow_ref[...] = jnp.where(low_half, scaled, 0.0).astype(BF16)
    xhigh_ref[...] = jnp.where(low_half, 0.0, scaled).astype(BF16)
    loads[3].wait()
    z_ref[...] = mm(normed_ref[...], wgate_ref[...])
    a_ref[...] = step * (jnp.exp(decay_ref[...]) * (-LOG2E))

    lane = iota((TILE, TILE), 1)
    for q in range(rows // TILE):
        here = slice(q * TILE, (q + 1) * TILE)
        keys = [slice(k * TILE, (k + 1) * TILE) for k in range(max(0, q - band), q + 1)]
        seg = seg_ref[here, :]
        row_at = iota((TILE, TILE), 0) + q * TILE
        c_rows = c_ref[here, :]
        scores = []
        cum = jnp.zeros((TILE, TILE), F32)
        for key in keys:
            at = lane + key.start
            valid = (at >= seg) & (at <= row_at)
            scores.append(jnp.where(valid, mm(c_rows, b_ref[key, :], NT), 0.0))
            ones = jnp.where(valid, 1.0, 0.0).astype(BF16)
            for piece in split3(a_ref[key, :]):
                cum = cum + mm(ones, piece)
        cumt_ref[here, :] = cum.T
        for pair in range(heads // 2):
            total = jnp.zeros((TILE, TILE), F32)
            columns = slice(pair * TILE, (pair + 1) * TILE)
            own = [
                jnp.broadcast_to(cum[:, h : h + 1], (TILE, TILE)) for h in (2 * pair, 2 * pair + 1)
            ]
            for key, score in zip(keys, scores):
                weights = [
                    (
                        jnp.exp2(jnp.minimum(own[half] - cumt_ref[key, :][h : h + 1, :], 0.0)) * score
                    ).astype(BF16)
                    for half, h in enumerate((2 * pair, 2 * pair + 1))
                ]
                values = jnp.concatenate([xlow_ref[key, columns], xhigh_ref[key, columns]], axis=0)
                total = total + mm(jnp.concatenate(weights, axis=1), values)
            y_ref[here, columns] = total

    gated = (y_ref[...] + skip_ref[...] * xs_ref[...].astype(F32)) * silu(z_ref[...])
    sq = gated * gated
    sq_high = sq.astype(BF16)
    sq_low = (sq - sq_high.astype(F32)).astype(BF16)
    ones = jnp.ones((EXTRA, inner), BF16)
    sums = mm(ones, sq_high, NT) + mm(ones, sq_low, NT)
    high, mid, low = split3(sums)
    row = iota(sums.shape, 0)
    zero = jnp.zeros(sums.shape, F32)
    message = jnp.where(
        row == 0,
        high.astype(F32),
        jnp.where(row == 1, mid.astype(F32), jnp.where(row == 2, low.astype(F32), zero)),
    ).astype(BF16)
    gn = (gated * ngain_ref[...]).astype(BF16)
    loads[4].wait()
    for k, out in enumerate(outs):
        columns = pl.ds(pl.multiple_of((part ^ k) * width, width), width)
        out[0:rows, :] = mm(gn, wout_ref[:, columns]).astype(BF16)
        out[rows : rows + EXTRA, :] = jnp.zeros((EXTRA, width), BF16)
        out[rows : rows + EXTRA, 0:rows] = message
    tail = rows + EXTRA
    outs[0][tail : tail + rows, :] = gn
    at = tail + rows
    for piece in blocks[0]:
        outs[0][at : at + piece.shape[0], :] = piece[...]
        at += piece.shape[0]


def sum_kernel(tensor, inner_all, rows, *refs):
    parts, outs, y_ref = refs[:tensor], refs[tensor:-1], refs[-1]
    width = parts[0].shape[1]
    tail = rows + EXTRA
    ones = jnp.ones((EXTRA, TILE), BF16)
    square = sum(mm(part[rows:tail, 0:rows], ones, TN) for part in parts)
    scale = lax.rsqrt(square * (1.0 / inner_all) + EPS)
    for c in range(0, width, TILE):
        columns = slice(c, c + TILE)
        total = sum(part[0:rows, columns].astype(F32) for part in parts)
        residual = parts[0][tail + rows : tail + 2 * rows, columns].astype(F32)
        result = (residual + total * scale).astype(BF16)
        size = rows // len(outs)
        for index, out_ref in enumerate(outs):
            out_ref[:, columns] = result[index * size : (index + 1) * size, :]
        y_ref[:, columns] = (parts[0][tail : tail + rows, columns].astype(F32) * scale).astype(BF16)


def half_kernel(pos_ref, own_ref, other_ref, out_ref):
    @pl.when(pos_ref[2] == 0)
    def _():
        out_ref[...] = other_ref[...]

    @pl.when(pos_ref[2] != 0)
    def _():
        out_ref[...] = own_ref[...]


def grad_kernel(active, pieces, pos_ref, *refs):
    ys, cot_ref, outs = refs[: -1 - pieces], refs[-1 - pieces], refs[-pieces:]
    width = outs[0].shape[1]

    @pl.when(pos_ref[2] == active)
    def _():
        for k, out in enumerate(outs):
            if pieces == 1:
                columns = slice(0, width)
            else:
                columns = pl.ds(pl.multiple_of((pos_ref[0] ^ k) * width, width), width)
            total, at = 0.0, 0
            for y in ys:
                rows = y.shape[0]
                total = total + mm(y[...], cot_ref[at : at + rows, columns], TN)
                at += rows
            out[...] = total.astype(BF16)


def total_kernel(encoder_count, pos_ref, *refs):
    encoder, decoder, out_ref = refs[:encoder_count], refs[encoder_count:-1], refs[-1]

    def add(terms):
        rows = terms[0].shape[0]
        for at in range(0, rows, TILE):
            total = sum(term[at : at + TILE, :].astype(F32) for term in terms)
            out_ref[0, at : at + TILE, :] = total.astype(BF16)

    @pl.when(pos_ref[2] == 0)
    def _():
        add(encoder)

    @pl.when(pos_ref[2] != 0)
    def _():
        add(decoder)


def assemble_kernel(counts, pos_ref, *refs):
    groups = []
    for count in counts:
        groups.append(refs[:count])
        refs = refs[count:]
    out_ref, sem = refs
    part = pos_ref[1]
    tensor = len(counts) // 2

    def move(blocks):
        copies = []
        for k, pieces in enumerate(blocks):
            at = 0
            for piece in pieces:
                rows, width = piece.shape
                columns = pl.ds(pl.multiple_of((part ^ k) * width, width), width)
                copies.append(
                    pltpu.make_async_copy(
                        piece, out_ref.at[0, at : at + rows, columns], sem.at[len(copies)]
                    )
                )
                at += rows
        for copy in copies:
            copy.start()
        for copy in copies:
            copy.wait()

    @pl.when(pos_ref[2] == 0)
    def _():
        move(groups[:tensor])

    @pl.when(pos_ref[2] != 0)
    def _():
        move(groups[tensor:])


def tensor_gather(value):
    count = lax.axis_size("tensor")
    return [
        lax.ppermute(value, "tensor", [(t, t ^ k) for t in range(count)]) for k in range(1, count)
    ]


def tensor_cross(values, active, first=0):
    count = lax.axis_size("tensor")
    other = 1 - active
    return [
        lax.ppermute(
            value,
            ("section", "tensor"),
            [(active * count + t, other * count + (t ^ k)) for t in range(count)]
            + [(other * count + t, active * count + t) for t in range(count)],
        )
        for k, value in enumerate(values, first)
    ]


def dp_cross(values, active, first):
    count = lax.axis_size("dp")
    other = 1 - active
    return [
        lax.ppermute(
            value,
            ("dp", "section"),
            [(d * 2 + active, (d ^ k) * 2 + other) for d in range(count)]
            + [(d * 2 + other, d * 2 + active) for d in range(count)],
        )
        for k, value in enumerate(values, first)
    ]


def per_device(
    tokens,
    base_rows,
    baseline_owner,
    cotangent,
    pre_gain,
    input_proj,
    gate_proj,
    state_proj,
    step_proj,
    step_bias,
    decay_log,
    skip_gain,
    norm_gain,
    out_proj,
):
    dp_count = lax.axis_size("dp")
    tensor = lax.axis_size("tensor")
    tok_rows, feat = tokens.shape
    cap = 2 * tok_rows // dp_count
    own_slots = cap * dp_count
    width = feat // tensor
    inner = input_proj.shape[2]
    heads = step_proj.shape[2]
    longest = 3 * tok_rows // base_rows.shape[0] * dp_count
    band = (longest - 1 + TILE - 1) // TILE
    dp_at = lax.axis_index("dp")
    section = lax.axis_index("section")
    pos = jnp.stack([dp_at, lax.axis_index("tensor"), section]).astype(jnp.int32)
    shape = jax.ShapeDtypeStruct
    tables = (pos, base_rows, baseline_owner)

    outgoing = pl.pallas_call(
        functools.partial(select_kernel, dp_count, cap),
        out_shape=[shape((cap, width), BF16)] * dp_count,
        in_specs=[smem()] * 3 + [pl.BlockSpec(memory_space=pl.ANY)],
        out_specs=[vmem()] * dp_count,
        scratch_shapes=[
            pltpu.VMEM((8, tok_rows), jnp.int32),
            pltpu.SMEM((dp_count,), jnp.int32),
            pltpu.VMEM((tok_rows, width), BF16),
            pltpu.SemaphoreType.DMA,
        ],
        compiler_params=params(),
        name="select_rows",
    )(*tables, tokens)
    swap = [(0, 1), (1, 0)]
    barrier = lax.optimization_barrier
    cot_own = cotangent[0]
    cot_other = lax.ppermute(cot_own, "section", swap)
    arrived = [outgoing[0]] + dp_cross(outgoing[1:], 0, 1)
    arrived, cot_other = barrier((arrived, cot_other))
    own_block, seg = pl.pallas_call(
        functools.partial(place_kernel, dp_count, cap),
        out_shape=[shape((own_slots, width), BF16), shape((own_slots, TILE), jnp.int32)],
        in_specs=[smem()] * 3 + [vmem()] * dp_count,
        out_specs=[vmem()] * 2,
        scratch_shapes=[
            pltpu.VMEM((8, own_slots), jnp.int32),
            pltpu.SMEM((dp_count,), jnp.int32),
            pltpu.VMEM((own_slots, width), BF16),
        ],
        compiler_params=params(),
        name="place_rows",
    )(*tables, *arrived)

    def lanes(value):
        return jnp.pad(value, ((0, 0), (0, TILE - heads)))

    weights = (
        pre_gain,
        input_proj[0],
        gate_proj[0],
        state_proj[0],
        lanes(step_proj[0]),
        lanes(step_bias),
        lanes(decay_log),
        jnp.repeat(skip_gain, HEADDIM, axis=1),
        norm_gain,
        out_proj[0],
    )

    is_large = [index in (1, 2, 3, 4, 9) for index in range(len(weights))]
    part_rows = [3 * own_slots + EXTRA] + [own_slots + EXTRA] * (tensor - 1)

    def layer(active, blocks):
        counts = tuple(len(pieces) for pieces in blocks)
        return pl.pallas_call(
            functools.partial(layer_kernel, active, counts, band),
            out_shape=[shape((count, width), BF16) for count in part_rows],
            in_specs=[smem()]
            + [vmem()] * (sum(counts) + 1)
            + [pl.BlockSpec(memory_space=pl.ANY) if large else vmem() for large in is_large],
            out_specs=[vmem()] * tensor,
            scratch_shapes=[
                pltpu.VMEM((own_slots, feat), BF16),
                pltpu.VMEM((own_slots, inner), BF16),
                pltpu.VMEM((own_slots, inner), F32),
                pltpu.VMEM((own_slots, NSTATE), BF16),
                pltpu.VMEM((own_slots, NSTATE), BF16),
                pltpu.VMEM((own_slots, TILE), F32),
                pltpu.VMEM((own_slots, TILE), F32),
                pltpu.VMEM((own_slots, inner), BF16),
                pltpu.VMEM((own_slots, inner), BF16),
                pltpu.VMEM((own_slots, inner), F32),
            ]
            + [pltpu.VMEM(weights[index].shape, BF16) for index in (3, 4, 1, 2, 9)]
            + [pltpu.SemaphoreType.DMA((5,))],
            compiler_params=params(),
            cost_estimate=cost(2 * own_slots * feat * (3 * inner + 512), 12e6),
            name="layer_part",
        )(pos, *[piece for pieces in blocks for piece in pieces], seg, *weights)

    def finish(parts, count):
        return pl.pallas_call(
            functools.partial(sum_kernel, tensor, inner * tensor, own_slots),
            out_shape=[shape((own_slots // count, width), BF16)] * count
            + [shape((own_slots, inner), BF16)],
            in_specs=[vmem()] * tensor,
            out_specs=[vmem()] * (count + 1),
            compiler_params=params(),
            cost_estimate=cost(1e6, 3e6),
            name="sum_parts",
        )(*parts)

    def gradient_terms(active, ys, cot, pieces):
        return pl.pallas_call(
            functools.partial(grad_kernel, active, pieces),
            out_shape=[shape((inner, feat // pieces), BF16)] * pieces,
            in_specs=[smem()] + [vmem()] * (len(ys) + 1),
            out_specs=[vmem()] * pieces,
            compiler_params=params(),
            cost_estimate=cost(2 * own_slots * inner * feat, 5e6),
            name="gradient_terms",
        )(pos, *ys, cot)

    direct = feat // dp_count % TILE == 0
    pieces = dp_count if direct else 1
    half = own_slots // 2

    blocks = [[value] for value in tensor_cross([own_block] * tensor, 1)]
    top, bottom, enc_y = finish(tensor_cross(layer(0, blocks), 0), 2)

    passed = lax.ppermute(bottom, "section", swap)
    mine = pl.pallas_call(
        half_kernel,
        out_shape=shape((half, width), BF16),
        in_specs=[smem()] + [vmem()] * 2,
        out_specs=vmem(),
        compiler_params=params(),
        cost_estimate=cost(1e5, 5e5),
        name="own_half",
    )(pos, top, passed)
    gathered = tensor_gather(mine)
    enc_y, gathered[0] = barrier((enc_y, gathered[0]))
    enc_terms = gradient_terms(1, [enc_y], cot_other, pieces)
    enc_terms, gathered = barrier((enc_terms, gathered))
    swapped = [lax.ppermute(value, "section", swap) for value in gathered]
    sources = [[top, bottom]] + [list(pair) for pair in zip(gathered, swapped)]
    kept = [list(pair) for pair in zip(swapped, gathered)]

    sources, enc_terms = barrier((sources, enc_terms))
    first = [k for k in range(1, dp_count) if k != dp_count // 2] if direct else []
    enc_grad = [dp_cross([enc_terms[k]], 1, k)[0] for k in first]
    parts, enc_grad, enc_terms = barrier((layer(1, sources), enc_grad, enc_terms))
    if direct:
        enc_grad = enc_grad + [dp_cross([enc_terms[k]], 1, k)[0] for k in (dp_count // 2, 0)]
    arrived = tensor_cross(parts, 1)
    top, arrived = barrier((top, arrived))
    kept = [[lax.ppermute(top, "section", swap), passed]] + kept
    rebuilt, dec_y = finish(arrived, 1)
    dec_terms = gradient_terms(0, [dec_y], cot_other, pieces)
    dec_terms, enc_grad = barrier((dec_terms, enc_grad))
    if direct:
        dec_grad = dp_cross(dec_terms, 0, 0)
    else:
        enc_grad, dec_grad = [
            [
                lax.ppermute(
                    lax.psum_scatter(terms[0], "dp", scatter_dimension=1, tiled=True), "section", swap
                )
            ]
            for terms in (enc_terms, dec_terms)
        ]
    rebuilt, dec_terms = barrier((rebuilt, dec_terms))
    finals = tensor_cross([rebuilt] * 2, 0)
    rebuilt, finals[0] = barrier((rebuilt, finals[0]))
    finals = [[value] for value in finals + tensor_cross([rebuilt] * (tensor - 2), 0, 2)]

    groups = kept + finals
    counts = tuple(len(group) for group in groups)
    activations = pl.pallas_call(
        functools.partial(assemble_kernel, counts),
        out_shape=shape((1, own_slots, feat), BF16),
        in_specs=[smem()] + [pl.BlockSpec(memory_space=pl.ANY)] * sum(counts),
        out_specs=pl.BlockSpec(memory_space=pl.ANY),
        scratch_shapes=[pltpu.SemaphoreType.DMA((2 * tensor,))],
        compiler_params=params(),
        cost_estimate=cost(1e6, 4e6),
        name="assemble_rows",
    )(pos, *[piece for group in groups for piece in group])
    out_grad = pl.pallas_call(
        functools.partial(total_kernel, len(enc_grad)),
        out_shape=shape((1, inner, feat // dp_count), BF16),
        in_specs=[smem()] + [vmem()] * (len(enc_grad) + len(dec_grad)),
        out_specs=vmem(),
        compiler_params=params(),
        cost_estimate=cost(1e6, 4e6),
        name="gradient_total",
    )(pos, *enc_grad, *dec_grad)
    return activations, out_grad


def solution(mesh):
    return jax.shard_map(
        per_device,
        mesh=mesh,
        in_specs=(
            P("dp", None),
            P(),
            P(),
            P("section", "dp", None),
            P("section", None),
            P("section", None, "tensor"),
            P("section", None, "tensor"),
            P("section", None, None),
            P("section", None, "tensor"),
            P("section", "tensor"),
            P("section", "tensor"),
            P("section", "tensor"),
            P("section", "tensor"),
            P("section", "tensor", None),
        ),
        out_specs=(P("section", "dp", None), P("section", "tensor", "dp")),
        check_vma=False,
    )
```
